768 devices in a mesh: mesh: 96 (over x, z, core), lev: 8 (over y).
Axes of the slice: x: 4, y: 8, z: 12, core: 2. Of those that a mesh axis runs over, the one named last changes fastest.
Arguments:
- velocity: float32 [16, 294912], P('lev', 'mesh'), may hold values from -6 to 6
- thickness: float32 [16, 294912], P('lev', 'mesh'), may hold values from 0.5 to 2
- vorticity: float32 [16, 294912], P('lev', 'mesh'), may hold values from -6 to 6
- vertical_wind: float32 [16, 294912], P('lev', 'mesh'), may hold values from -6 to 6
- weights_on_edge: float32 [10, 294912], P(None, 'mesh'), may hold values from -2 to 2
- edges_on_edge: int32 [10, 294912], P(None, 'mesh'), may hold values from 0 to 3839, as said below
- edges_on_cell: int32 [6, 98304], P(None, 'mesh'), may hold values from 0 to 3839, as said below
- cells_on_edge: int32 [2, 294912], P(None, 'mesh'), may hold values from 0 to 1407, as said below
- energy_weight: float32 [6, 98304], P(None, 'mesh'), may hold values from 0.05 to 0.5
- inverse_distance: float32 [294912], P('mesh'), may hold values from 0.5 to 2
- edge_halo_list: int32 [576, 128], P('mesh'), may hold values from 0 to 3071
- edge_halo_count: int32 [576], P('mesh'), may hold values from 1 to 128, as said below
- cell_halo_list: int32 [576, 64], P('mesh'), may hold values from 0 to 1023
- cell_halo_count: int32 [576], P('mesh'), may hold values from 1 to 64, as said below
Outputs:
- tendency: float32 [16, 294912], P('lev', 'mesh')
- tangent: float32 [16, 294912], P('lev', 'mesh')
- energy: float32 [16, 98304], P('lev', 'mesh')
The draws below stay inside these ranges and needn't reach their ends.
Inputs may be any that keep to these rules, and one draw needn't show every extreme that they name: `edge_halo_count`: row r names how many leading slots of the halo block r are live. `cell_halo_count`: row r names how many leading slots of the halo block r are live. `edges_on_edge`: entries name local edges or live slots of edge halo blocks. `edges_on_cell`: entries name local edges or live slots of edge halo blocks. `cells_on_edge`: entries name local cells or live slots of cell halo blocks.
All inputs are finite; a program needn't handle non-finite values.
Results may differ from the reference program's by a relative error of at most 0.0003.
Values sent between devices are 32-bit elements; how exact they have to be, the bound alone decides.
No kernel may reach another device: no remote copies, remote signals or barrier semaphores. Data moves between devices by JAX's collectives and lax.ppermute only.
A program may use at most 128 MiB of HBM per device.

```python
import math
import jax
import jax.numpy as jnp
from jax import lax

C_DEV = 1024
E_DEV = 3072
NEOE = 10
NEOC = 6
REACH = 3
HALO_E = 128
HALO_C = 64
NBLOCK = 6
NLEV = 16
EDGES = 294912
CELLS = 98304
N_MESH = 96


def offsets_table_drawn():
    order = jnp.arange(NBLOCK, dtype=jnp.int32)
    return jnp.where(order < REACH, order + 1, REACH - 1 - order).astype(jnp.int32)


def halo_counts(key, salt, most):
    inner = jax.random.fold_in(key, salt)
    first, second = jax.random.split(inner)
    counts = jax.random.randint(first, (N_MESH * NBLOCK,), 1, most + 1)
    sender = jax.random.randint(second, (), 0, N_MESH)
    full_row = sender * NBLOCK + NBLOCK - 1
    counts = jnp.where(jnp.arange(N_MESH * NBLOCK) == full_row, most, counts)
    return (counts.astype(jnp.int32), sender)


def halo_refs(key, total, local_size, column_size, counts, sender, most, leading):
    keys = jax.random.split(key, 4)
    owner = (jnp.arange(total, dtype=jnp.int32) // column_size)[None, :]
    local_pick = jax.random.randint(keys[0], (leading, total), 0, local_size)
    block = jax.random.randint(keys[1], (leading, total), 0, NBLOCK)
    raw_slot = jax.random.randint(keys[2], (leading, total), 0, 1 << 20)
    remote = jax.random.randint(keys[3], (leading, total), 0, 4) == 0
    source = (owner - offsets_table_drawn()[block]) % N_MESH
    live = counts[source * NBLOCK + block]
    slot = raw_slot % live
    table = jnp.where(remote, local_size + block * most + slot, local_pick)
    receiver = (sender - REACH) % N_MESH
    spot = (jnp.arange(leading)[:, None] == 0) & (jnp.arange(total)[None, :] == receiver * column_size)
    table = jnp.where(spot, local_size + NBLOCK * most - 1, table)
    return table.astype(jnp.int32)


def bounded_list(key, rows, breadth, top):
    keys = jax.random.split(key, 3)
    values = jax.random.randint(keys[0], (rows * breadth,), 0, top)
    high_spot = jax.random.randint(keys[1], (), 0, rows * breadth)
    low_spot = (high_spot + 1 + jax.random.randint(keys[2], (), 0, rows * breadth - 1)) % (rows * breadth)
    places = jnp.arange(rows * breadth)
    values = jnp.where(places == high_spot, top - 1, values)
    values = jnp.where(places == low_spot, 0, values)
    return values.reshape(rows, breadth).astype(jnp.int32)


def draw_edge_halo_count(key, part):
    counts, sender = halo_counts(key, 11, HALO_E)
    return counts


def draw_cell_halo_count(key, part):
    counts, sender = halo_counts(key, 12, HALO_C)
    return counts


def draw_edge_halo_list(key, part):
    key = jax.random.fold_in(key, 21)
    return bounded_list(key, N_MESH * NBLOCK, HALO_E, E_DEV)


def draw_cell_halo_list(key, part):
    key = jax.random.fold_in(key, 22)
    return bounded_list(key, N_MESH * NBLOCK, HALO_C, C_DEV)


def draw_edges_on_edge(key, part):
    counts, sender = halo_counts(key, 11, HALO_E)
    key = jax.random.fold_in(key, 31)
    return halo_refs(key, EDGES, E_DEV, E_DEV, counts, sender, HALO_E, NEOE)


def draw_edges_on_cell(key, part):
    counts, sender = halo_counts(key, 11, HALO_E)
    key = jax.random.fold_in(key, 32)
    return halo_refs(key, CELLS, E_DEV, C_DEV, counts, sender, HALO_E, NEOC)


def draw_cells_on_edge(key, part):
    counts, sender = halo_counts(key, 12, HALO_C)
    key = jax.random.fold_in(key, 33)
    return halo_refs(key, EDGES, C_DEV, E_DEV, counts, sender, HALO_C, 2)


def block_levels(key, shape, pieces, smallest, top_value):
    loudness = 1.0
    for position, shards_of in pieces:
        draws = jax.random.uniform(jax.random.fold_in(jax.random.fold_in(key, 6), position), (shards_of,), jnp.float32, smallest / len(pieces), top_value / len(pieces))
        loudness = loudness * jnp.repeat(jnp.exp(draws), shape[position] // shards_of).reshape((-1,) + (1,) * (len(shape) - 1 - position))
    return loudness


def normal_values(stream_key, dims, width, most, cuts=(), kind=jnp.bfloat16):
    array = jax.random.normal(stream_key, dims, jnp.float32) * width
    if len(cuts) > 0:
        array = block_levels(stream_key, dims, cuts, -0.22, 0.18) * array
    return jnp.clip(array, min=-most, max=most).astype(kind)


def setup_inputs(seed: int = 0) -> dict:
    key_of = jax.random.split(jax.random.key(seed), 15)
    return {
        "velocity": normal_values(key_of[0], (NLEV, EDGES), 1.0, 6.0, ((0, 8), (1, 96)), jnp.float32),
        "thickness": jnp.clip(jnp.exp(math.log(2.0) - 1.3862944 * jax.random.uniform(key_of[1], (NLEV, EDGES), jnp.float32) ** block_levels(key_of[1], (NLEV, EDGES), ((0, 8), (1, 96)), -0.2, 0.2)), 0.5, 2.0),
        "vorticity": normal_values(key_of[2], (NLEV, EDGES), 1.0, 6.0, ((0, 8), (1, 96)), jnp.float32),
        "vertical_wind": normal_values(key_of[3], (NLEV, EDGES), 1.0, 6.0, ((0, 8), (1, 96)), jnp.float32),
        "weights_on_edge": normal_values(key_of[4], (NEOE, EDGES), NEOE ** -0.5, 2.0, ((1, 96),), jnp.float32),
        "edges_on_edge": draw_edges_on_edge(jax.random.fold_in(key_of[14], 71), 0),
        "edges_on_cell": draw_edges_on_cell(jax.random.fold_in(key_of[14], 71), 0),
        "cells_on_edge": draw_cells_on_edge(jax.random.fold_in(key_of[14], 71), 0),
        "energy_weight": jnp.clip(jnp.exp(math.log(0.5) - 2.3025851 * jax.random.uniform(key_of[8], (NEOC, CELLS), jnp.float32) ** block_levels(key_of[8], (NEOC, CELLS), ((1, 96),), -0.2, 0.2)), 0.05, 0.5),
        "inverse_distance": jnp.clip(jnp.exp(math.log(2.0) - 1.3862944 * jax.random.uniform(key_of[9], (EDGES,), jnp.float32) ** block_levels(key_of[9], (EDGES,), ((0, 96),), -0.2, 0.2)), 0.5, 2.0),
        "edge_halo_list": draw_edge_halo_list(jax.random.fold_in(key_of[14], 71), 0),
        "edge_halo_count": draw_edge_halo_count(jax.random.fold_in(key_of[14], 71), 0),
        "cell_halo_list": draw_cell_halo_list(jax.random.fold_in(key_of[14], 71), 0),
        "cell_halo_count": draw_cell_halo_count(jax.random.fold_in(key_of[14], 71), 0),
    }


def offsets_table():
    order = jnp.arange(NBLOCK, dtype=jnp.int32)
    return jnp.where(order < REACH, order + 1, REACH - 1 - order).astype(jnp.int32)


def resolve(table, local_size, column_size, halo_list, halo_count, breadth):
    total = table.shape[-1]
    owner = (jnp.arange(total, dtype=jnp.int32) // column_size)[None, :]
    slot = jnp.maximum(table - local_size, 0)
    block = slot // breadth
    place = slot % breadth
    sender = (owner - offsets_table()[block]) % N_MESH
    row = (sender * NBLOCK + block).astype(jnp.int32)
    remote_item = sender * local_size + halo_list[row, place]
    remote = table >= local_size
    index = jnp.where(remote, remote_item, owner * local_size + table).astype(jnp.int32)
    keep = jnp.where(remote, place < halo_count[row], True)
    return index, keep


def reference(velocity, thickness, vorticity, vertical_wind, weights_on_edge, edges_on_edge, edges_on_cell, cells_on_edge, energy_weight, inverse_distance, edge_halo_list, edge_halo_count, cell_halo_list, cell_halo_count):
    near_edges, near_keep = resolve(edges_on_edge, E_DEV, E_DEV, edge_halo_list, edge_halo_count, HALO_E)
    cell_edges, cell_keep = resolve(edges_on_cell, E_DEV, C_DEV, edge_halo_list, edge_halo_count, HALO_E)
    end_cells, end_keep = resolve(cells_on_edge, C_DEV, E_DEV, cell_halo_list, cell_halo_count, HALO_C)

    def level_terms(row):
        speed, height, potential = row
        speed_near = jnp.where(near_keep, speed[near_edges], 0.0)
        height_near = jnp.where(near_keep, height[near_edges], 0.0)
        potential_near = jnp.where(near_keep, potential[near_edges], 0.0)
        tangent_row = jnp.sum(weights_on_edge * speed_near, axis=0)
        flux_row = jnp.sum(weights_on_edge * speed_near * height_near * 0.5 * (potential[None, :] + potential_near), axis=0)
        cell_speed = jnp.where(cell_keep, speed[cell_edges], 0.0)
        energy_row = jnp.sum(energy_weight * cell_speed * cell_speed, axis=0)
        ends = jnp.where(end_keep, energy_row[end_cells], 0.0)
        gradient_row = (ends[1] - ends[0]) * inverse_distance
        return flux_row - gradient_row, tangent_row, energy_row

    partial_sum, tangent, energy = lax.map(level_terms, (velocity, thickness, vorticity))
    zero_row = jnp.zeros_like(velocity[:1])
    above = jnp.concatenate([velocity[1:], zero_row], axis=0)
    below = jnp.concatenate([zero_row, velocity[:-1]], axis=0)
    advect = -0.5 * vertical_wind * (above - below)
    return partial_sum + advect, tangent, energy
```

```python
import jax
import jax.numpy as jnp
from jax import lax
from jax.experimental import pallas as pl
from jax.experimental.pallas import tpu as pltpu
from jax.sharding import Mesh, PartitionSpec as P

OFF = (1, 2, 3, -1, -2, -3)
LANES = 128
ROWS = 24
LOCAL = ROWS * LANES
BLOCKS = 8

WAY = 6
RIM = 2 * WAY
TILES = RIM + 6
NEAR, MIDDLE, FAR, EDGE = 0, 12, 18, 22


def pick(table, low):
    return jnp.take_along_axis(table, low, axis=1, mode="promise_in_bounds")


def wide(row):
    return jnp.broadcast_to(row, (8, LANES))


def sublanes():
    return lax.broadcasted_iota(jnp.int32, (8, LANES), 0)


def total(tile):
    return jnp.sum(tile, axis=0, keepdims=True)


def halves(left, right):
    lane = lax.broadcasted_iota(jnp.int32, left.shape, 1)
    return jnp.where(lane < 64, left, right)


def turn(tile):
    return pltpu.roll(tile, 64, 1)


def pack_kernel(
    speed_hbm, height_hbm, vort_hbm, edge_list_hbm, cell_list_hbm, cells_hbm, share_hbm,
    sent_ref, table_ref,
    speed_ref, height_ref, vort_ref, edge_list_ref, cell_list_ref, cells_ref, share_ref, pair_ref, done,
):
    pairs = (
        (speed_hbm, speed_ref), (height_hbm, height_ref), (vort_hbm, vort_ref), (edge_list_hbm, edge_list_ref),
        (cell_list_hbm, cell_list_ref), (cells_hbm, cells_ref), (share_hbm, share_ref),
    )
    copies = [pltpu.make_async_copy(src, dst, done.at[i]) for i, (src, dst) in enumerate(pairs)]
    for copy in copies:
        copy.start()
    for copy in copies:
        copy.wait()
    for level in range(2):
        for row in range(ROWS):
            tile, place = level * 3 + row // 8, slice(row % 8, row % 8 + 1)
            columns = slice(row * LANES, (row + 1) * LANES)
            table_ref[tile, place, :] = speed_ref[level : level + 1, columns]
            table_ref[6 + tile, place, :] = height_ref[level : level + 1, columns]
            table_ref[12 + tile, place, :] = vort_ref[level : level + 1, columns]
    for tile in range(6):
        speed = table_ref[tile]
        mass = speed * table_ref[6 + tile]
        table_ref[6 + tile] = mass
        table_ref[12 + tile] = mass * table_ref[12 + tile]
        sent_ref[RIM + tile] = speed
    for way in range(2):
        for tile in (0, 1, 5):
            sent_ref[way * WAY + tile] = jnp.zeros((8, LANES), jnp.float32)
    spot = sublanes()
    for block in range(6):
        index = wide(edge_list_ref[block : block + 1, :])
        low, high = index & 127, index >> 7
        way, place = WAY * (block // 3), block % 3
        for field in range(6):
            found = jnp.zeros((8, LANES), jnp.float32)
            for part in range(3):
                got = pick(table_ref[field * 3 + part], low)
                found = jnp.where(high == spot + 8 * part, got, found)
            row, level = total(found), field % 2
            if field < 2:
                sent_ref[level, block : block + 1, :] = row
                sent_ref[WAY + level, block : block + 1, :] = row
            elif field < 4:
                sent_ref[way + 2 + place, 6 + level : 7 + level, :] = row
            else:
                sent_ref[way + 5, level * 3 + place : level * 3 + place + 1, :] = row
    pair_ref[...] = jnp.zeros((8, LANES), jnp.int32)
    for block in range(6):
        pair_ref[block : block + 1, 0:64] = cell_list_ref[block : block + 1, :]
    lists = pair_ref[...]
    turned = turn(lists)
    for group in range(3):
        index = wide(lists[2 * group : 2 * group + 1] + turned[2 * group + 1 : 2 * group + 2])
        low, high = index[:6] & 127, index[:6] >> 7
        edges = jnp.zeros((6, LANES), jnp.int32)
        shares = jnp.zeros((6, LANES), jnp.float32)
        for block in range(BLOCKS):
            columns = slice(block * LANES, (block + 1) * LANES)
            here = high == block
            edges = jnp.where(here, pick(cells_ref[:, columns], low), edges)
            shares = jnp.where(here, pick(share_ref[:, columns], low), shares)
        names = (edges - LOCAL).astype(jnp.float32)
        tables = (halves(names, turn(shares)), halves(turn(names), shares))
        sums = [jnp.zeros((8, LANES), jnp.float32) for _ in range(2)]
        for side in range(6):
            index, share = wide(edges[side : side + 1]), wide(shares[side : side + 1])
            low, high = index & 127, index >> 7
            for part in range(3):
                weight = jnp.where(high == spot + 8 * part, share, 0.0)
                for level in range(2):
                    got = pick(table_ref[level * 3 + part], low)
                    sums[level] = sums[level] + weight * (got * got)
        sums = [total(part) for part in sums]
        parts = (halves(sums[0], turn(sums[1])), halves(turn(sums[0]), sums[1]))
        for half in range(2):
            block = 2 * group + half
            way, place = WAY * (block // 3), block % 3
            sent_ref[way + 2 + place, 0:6, :] = tables[half]
            row = 6 + place % 2
            sent_ref[way + place // 2, row : row + 1, :] = parts[half]


def local_kernel(
    table_ref, near_ref, weight_ref, cells_ref, share_ref, sums_ref, energy_ref,
):
    spot = sublanes()
    table = table_ref[...].reshape(18 * 8, LANES)
    coarse = table.astype(jnp.bfloat16)
    fine = (table - coarse.astype(jnp.float32)).astype(jnp.bfloat16)
    table = jnp.concatenate([coarse, fine], axis=1)
    span = 2 * LANES
    counts = lax.broadcasted_iota(jnp.int32, (LANES, span), 0).astype(jnp.float32).astype(jnp.bfloat16)
    rows = lax.broadcasted_iota(jnp.int32, (8, span), 0)

    def edges(step, carry):
        columns = pl.ds(pl.multiple_of(step * span, span), span)
        sums = [jnp.zeros((8, span), jnp.float32) for _ in range(6)]
        for side in range(10):
            index = near_ref[side : side + 1, columns]
            weight = jnp.broadcast_to(weight_ref[side : side + 1, columns], (8, span))
            low = (index & 127).astype(jnp.float32).astype(jnp.bfloat16)
            high = jnp.broadcast_to(index >> 7, (8, span))
            ones = jnp.where(
                counts == jnp.broadcast_to(low, (LANES, span)), jnp.bfloat16(1), jnp.bfloat16(0)
            )
            got = jnp.dot(table, jnp.concatenate([ones, ones], axis=0), preferred_element_type=jnp.float32)
            for part in range(3):
                here = jnp.where(high == rows + 8 * part, weight, 0.0)
                for field in range(6):
                    row = (field * 3 + part) * 8
                    sums[field] = sums[field] + here * got[row : row + 8]
        for field in range(6):
            for half in range(2):
                sums_ref[step * 2 + half, field] = sums[field][:, half * LANES : (half + 1) * LANES]
        return carry

    lax.fori_loop(0, ROWS // 2, edges, 0, unroll=True)

    def cells(step, carry):
        columns = pl.ds(pl.multiple_of(step * LANES, LANES), LANES)
        sums = [jnp.zeros((8, LANES), jnp.float32) for _ in range(2)]
        for side in range(6):
            index = wide(cells_ref[side : side + 1, columns])
            share = wide(share_ref[side : side + 1, columns])
            low, high = index & 127, index >> 7
            for part in range(3):
                here = jnp.where(high == spot + 8 * part, share, 0.0)
                for level in range(2):
                    got = pick(table_ref[level * 3 + part], low)
                    sums[level] = sums[level] + here * (got * got)
        for level in range(2):
            energy_ref[step, level] = sums[level]
        return carry

    lax.fori_loop(0, BLOCKS, cells, 0, unroll=4)


def finish_kernel(
    core_ref, own_ref, around_ref, sums_ref, energy_sums_ref, near_ref, weight_ref, cells_ref, share_ref,
    ends_ref, inverse_ref, vort_ref, wind_ref, speed_ref, tendency_ref, tangent_ref, energy_ref,
    halo_ref, cell_ref,
):
    core = core_ref[0]
    first = jnp.full((8, LANES), core, jnp.int32) == 0
    spot = sublanes()

    def rows_at(way, tile, rows, place):
        chip, part = place // 2, place % 2
        side = 0 if chip < 0 else 1
        if chip == 0:
            return own_ref[part, way * WAY + tile, rows, :]
        if abs(chip) == 1:
            at = NEAR + part * WAY + tile
        elif abs(chip) == 2 and tile < 2:
            at = MIDDLE + part * 2 + tile
        elif abs(chip) == 2:
            assert part == 1 - side and tile >= 4
            at = MIDDLE + tile
        else:
            assert abs(chip) == 3 and tile < 2
            at = FAR + part * 2 + tile
        return around_ref[side, at, rows, :]

    def rows_of(distance, way, tile, start, stop):
        rows = slice(start, stop)
        on_first = rows_at(way, tile, rows, distance)
        on_second = rows_at(way, tile, rows, distance + 1)
        return jnp.where(first[: stop - start], on_first, on_second)

    for field in range(6):
        halo_ref[field] = jnp.zeros((8, LANES), jnp.float32)
    for block in range(6):
        away, way, place = -OFF[block], block // 3, block % 3
        mass = rows_of(away, way, 2 + place, 6, 8)
        for level in range(2):
            row = slice(block, block + 1)
            halo_ref[level, row, :] = rows_of(away, way, level, block, block + 1)
            halo_ref[2 + level, row, :] = mass[level : level + 1]
            at = level * 3 + place
            halo_ref[4 + level, row, :] = rows_of(away, way, 5, at, at + 1)

    squares = [halo_ref[level] * halo_ref[level] for level in range(2)]
    for step in range(BLOCKS):
        columns = slice(step * LANES, (step + 1) * LANES)
        sums = [energy_sums_ref[step, level] for level in range(2)]
        for side in range(6):
            index = wide(cells_ref[side : side + 1, columns])
            share = wide(share_ref[side : side + 1, columns])
            low, high = index & 127, index >> 7
            here = jnp.where(high == spot + ROWS, share, 0.0)
            for level in range(2):
                sums[level] = sums[level] + here * pick(squares[level], low)
        for level in range(2):
            row = total(sums[level])
            energy_ref[level : level + 1, columns] = row
            cell_ref[level, step : step + 1, :] = row

    for level in range(2):
        cell_ref[2 + level] = jnp.zeros((8, LANES), jnp.float32)
    for group in range(3):
        tables, names, parts = [], [], []
        for half in range(2):
            block = 2 * group + half
            away, way, place = -OFF[block], block // 3, block % 3
            for level in range(2):
                table = jnp.zeros((8, LANES), jnp.float32)
                for sender in range(6):
                    table = jnp.where(spot == sender, rows_of(away - OFF[sender], 0, level, 0, 8), table)
                tables.append(table * table)
            names.append(rows_of(away, way, 2 + place, 0, 8))
            row = 6 + place % 2
            parts.append(rows_of(away, way, place // 2, row, row + 1))
        indices = halves(names[0], turn(names[1])).astype(jnp.int32)
        shares = halves(turn(names[0]), names[1])
        parts = (halves(parts[0], turn(parts[1])), halves(turn(parts[0]), parts[1]))
        sums = [jnp.zeros((8, LANES), jnp.float32) for _ in range(2)]
        for side in range(6):
            index, share = wide(indices[side : side + 1]), wide(shares[side : side + 1])
            low, high = index & 127, index >> 7
            here = jnp.where(high == spot, share, 0.0)
            for level in range(2):
                got = halves(pick(tables[level], low), pick(tables[2 + level], low))
                sums[level] = sums[level] + here * got
        for level in range(2):
            cell_ref[2 + level, group : group + 1, :] = total(sums[level]) + parts[level]

    def edges(step, carry):
        columns = pl.ds(pl.multiple_of(step * LANES, LANES), LANES)
        sums = [sums_ref[step, field] for field in range(6)]
        for side in range(10):
            index = wide(near_ref[side : side + 1, columns])
            weight = wide(weight_ref[side : side + 1, columns])
            low, high = index & 127, index >> 7
            here = jnp.where(high == spot + ROWS, weight, 0.0)
            for field in range(6):
                sums[field] = sums[field] + here * pick(halo_ref[field], low)
        slopes = [jnp.zeros((8, LANES), jnp.float32) for _ in range(2)]
        for side in range(2):
            sign = 1.0 if side == 1 else -1.0
            index = wide(ends_ref[side : side + 1, columns])
            low, high = index & 127, index >> 7
            for part in range(2):
                here = high == spot + BLOCKS * part
                for level in range(2):
                    got = jnp.where(here, pick(cell_ref[2 * part + level], low), 0.0)
                    slopes[level] = slopes[level] + sign * got
        inverse = wide(inverse_ref[:, columns])
        row, tile = step % 8, step // 8
        below = around_ref[0, EDGE + core * 3 + tile, pl.ds(row, 1), :]
        above = around_ref[1, EDGE + core * 3 + tile, pl.ds(row, 1), :]
        speeds = [speed_ref[level : level + 1, columns] for level in range(2)]
        risers = [speeds[1] - below, above - speeds[0]]
        for level in range(2):
            vort = wide(vort_ref[level : level + 1, columns])
            flux = 0.5 * (vort * sums[2 + level] + sums[4 + level])
            result = total(flux - slopes[level] * inverse)
            advect = -0.5 * wind_ref[level : level + 1, columns] * risers[level]
            tendency_ref[level : level + 1, columns] = result + advect
            tangent_ref[level : level + 1, columns] = total(sums[level])
        return carry

    lax.fori_loop(0, ROWS, edges, 0, unroll=6)


VMEM = pl.BlockSpec(memory_space=pltpu.VMEM)


def body(
    velocity,
    thickness,
    vorticity,
    vertical_wind,
    weights_on_edge,
    edges_on_edge,
    edges_on_cell,
    cells_on_edge,
    energy_weight,
    inverse_distance,
    edge_halo_list,
    edge_halo_count,
    cell_halo_list,
    cell_halo_count,
):
    del edge_halo_count, cell_halo_count
    f32 = jnp.float32
    core = lax.axis_index("core")
    params = pltpu.CompilerParams(vmem_limit_bytes=24 << 20)
    inputs = (
        velocity, thickness, vorticity, edge_halo_list, cell_halo_list, edges_on_cell, energy_weight
    )
    sent, tables = pl.pallas_call(
        pack_kernel,
        out_shape=(
            jax.ShapeDtypeStruct((TILES, 8, LANES), f32),
            jax.ShapeDtypeStruct((18, 8, LANES), f32),
        ),
        in_specs=[pl.BlockSpec(memory_space=pltpu.HBM)] * 7,
        out_specs=(VMEM, VMEM),
        scratch_shapes=[pltpu.VMEM(x.shape, x.dtype) for x in inputs]
        + [pltpu.VMEM((8, LANES), jnp.int32), pltpu.SemaphoreType.DMA((7,))],
        compiler_params=pltpu.CompilerParams(vmem_limit_bytes=60 << 20),
        name="pack",
    )(*inputs)

    mesh_axes = ("x", "z", "core")
    own = lax.all_gather(sent, "core")
    even = core == 0
    near = jnp.where(even, own[:, :WAY], own[:, WAY:RIM])
    rims = jnp.where(even, own[:, RIM + 3 :], own[:, RIM : RIM + 3])
    chips = lax.axis_size("x") * lax.axis_size("z")

    def apart(block, distance):
        right = [(2 * c, 2 * ((c + distance) % chips)) for c in range(chips)]
        left = [(2 * c + 1, 2 * ((c - distance) % chips) + 1) for c in range(chips)]
        return lax.ppermute(block, mesh_axes, right + left)

    groups = lax.axis_size("lev")
    up = [(i, i + 1) for i in range(groups - 1)]
    down = [(groups + i + 1, groups + i) for i in range(groups - 1)]
    speeds = near[:, :2].reshape(4, 8, LANES)
    rest = jnp.where(even, near[1, 4:], near[0, 4:])
    arrived = [
        apart(near, 1).reshape(12, 8, LANES),
        apart(jnp.concatenate([speeds, rest], axis=0), 2),
        apart(speeds, 3),
        lax.ppermute(rims, ("core", "lev"), up + down).reshape(6, 8, LANES),
    ]
    arrived = jnp.concatenate(arrived, axis=0)
    sums, energy_sums = pl.pallas_call(
        local_kernel,
        out_shape=(
            jax.ShapeDtypeStruct((ROWS, 6, 8, LANES), f32),
            jax.ShapeDtypeStruct((BLOCKS, 2, 8, LANES), f32),
        ),
        in_specs=[VMEM] * 5,
        out_specs=(VMEM, VMEM),
        compiler_params=params,
        cost_estimate=pl.CostEstimate(flops=20_000_000, bytes_accessed=1_000_000, transcendentals=0),
        name="local",
    )(tables, edges_on_edge, weights_on_edge, edges_on_cell, energy_weight)
    around = lax.all_gather(arrived, "core")
    return pl.pallas_call(
        finish_kernel,
        out_shape=(
            jax.ShapeDtypeStruct(velocity.shape, f32),
            jax.ShapeDtypeStruct(velocity.shape, f32),
            jax.ShapeDtypeStruct((velocity.shape[0], edges_on_cell.shape[1]), f32),
        ),
        in_specs=[pl.BlockSpec(memory_space=pltpu.SMEM)] + [VMEM] * 13,
        out_specs=(VMEM, VMEM, VMEM),
        scratch_shapes=[pltpu.VMEM((6, 8, LANES), f32), pltpu.VMEM((4, 8, LANES), f32)],
        compiler_params=params,
        name="finish",
    )(
        core.astype(jnp.int32).reshape(1), own, around, sums, energy_sums, edges_on_edge, weights_on_edge,
        edges_on_cell, energy_weight, cells_on_edge, inverse_distance.reshape(1, -1), vorticity,
        vertical_wind, velocity,
    )


def solution(mesh):
    fine = Mesh(mesh.devices.reshape(4, 12, 2, 8), ("x", "z", "core", "lev"))
    parts = ("x", "z", "core")
    in_specs = (
        P("lev", parts),
        P("lev", parts),
        P("lev", parts),
        P("lev", parts),
        P(None, parts),
        P(None, parts),
        P(None, parts),
        P(None, parts),
        P(None, parts),
        P(parts),
        P(parts, None),
        P(parts),
        P(parts, None),
        P(parts),
    )
    out_specs = (P("lev", parts), P("lev", parts), P("lev", parts))
    return jax.shard_map(body, mesh=fine, in_specs=in_specs, out_specs=out_specs, check_vma=False)
```

```python
import jax
import jax.numpy as jnp
from jax import lax
from jax.experimental import pallas as pl
from jax.experimental.pallas import tpu as pltpu
from jax.sharding import Mesh, PartitionSpec as P

OFF = (1, 2, 3, -1, -2, -3)
LANES = 128
ROWS = 24
LOCAL = ROWS * LANES
BLOCKS = 8

WAY = 6
RIM = 2 * WAY
TILES = RIM + 6
NEAR, MIDDLE, FAR, EDGE = 0, 12, 19, 27


def pick(table, low):
    return jnp.take_along_axis(table, low, axis=1, mode="promise_in_bounds")


def wide(row):
    return jnp.broadcast_to(row, (8, LANES))


def sublanes():
    return lax.broadcasted_iota(jnp.int32, (8, LANES), 0)


def total(tile):
    return jnp.sum(tile, axis=0, keepdims=True)


SPAN = 2 * LANES
PRODUCTS = 9


def split(table, axis):
    coarse = table.astype(jnp.bfloat16)
    fine = (table - coarse.astype(jnp.float32)).astype(jnp.bfloat16)
    return jnp.concatenate([coarse, fine], axis=axis)


def ones_at(index, counts):
    low = (index & 127).astype(jnp.float32).astype(jnp.bfloat16)
    here = counts == jnp.broadcast_to(low, (LANES, SPAN))
    return jnp.where(here, jnp.bfloat16(1), jnp.bfloat16(0))


def product(table, ones):
    return jnp.dot(table, ones, preferred_element_type=jnp.float32)


def counting():
    return lax.broadcasted_iota(jnp.int32, (LANES, SPAN), 0).astype(jnp.float32).astype(jnp.bfloat16)


def halves(left, right):
    lane = lax.broadcasted_iota(jnp.int32, left.shape, 1)
    return jnp.where(lane < 64, left, right)


def turn(tile):
    return pltpu.roll(tile, 64, 1)


def pack_kernel(
    speed_hbm, height_hbm, vort_hbm, edge_list_hbm, cell_list_hbm, cells_hbm, share_hbm,
    sent_ref, table_ref,
    speed_ref, height_ref, vort_ref, edge_list_ref, cell_list_ref, cells_ref, share_ref, pair_ref, done,
):
    pairs = (
        (speed_hbm, speed_ref), (height_hbm, height_ref), (vort_hbm, vort_ref), (edge_list_hbm, edge_list_ref),
        (cell_list_hbm, cell_list_ref), (cells_hbm, cells_ref), (share_hbm, share_ref),
    )
    copies = [pltpu.make_async_copy(src, dst, done.at[i]) for i, (src, dst) in enumerate(pairs)]
    for copy in copies:
        copy.start()
    for copy in copies:
        copy.wait()
    for level in range(2):
        for row in range(ROWS):
            tile, place = level * 3 + row // 8, slice(row % 8, row % 8 + 1)
            columns = slice(row * LANES, (row + 1) * LANES)
            table_ref[tile, place, :] = speed_ref[level : level + 1, columns]
            table_ref[6 + tile, place, :] = height_ref[level : level + 1, columns]
            table_ref[12 + tile, place, :] = vort_ref[level : level + 1, columns]
    for tile in range(6):
        speed = table_ref[tile]
        mass = speed * table_ref[6 + tile]
        table_ref[6 + tile] = mass
        table_ref[12 + tile] = mass * table_ref[12 + tile]
        sent_ref[RIM + tile] = speed
    for way in range(2):
        for tile in (0, 1, 5):
            sent_ref[way * WAY + tile] = jnp.zeros((8, LANES), jnp.float32)
    spot = sublanes()
    for block in range(6):
        index = wide(edge_list_ref[block : block + 1, :])
        low, high = index & 127, index >> 7
        way, place = WAY * (block // 3), block % 3
        for field in range(6):
            found = jnp.zeros((8, LANES), jnp.float32)
            for part in range(3):
                got = pick(table_ref[field * 3 + part], low)
                found = jnp.where(high == spot + 8 * part, got, found)
            row, level = total(found), field % 2
            if field < 2:
                sent_ref[level, block : block + 1, :] = row
                sent_ref[WAY + level, block : block + 1, :] = row
            elif field < 4:
                sent_ref[way + 2 + place, 6 + level : 7 + level, :] = row
            else:
                sent_ref[way + 5, level * 3 + place : level * 3 + place + 1, :] = row
    pair_ref[...] = jnp.zeros((8, LANES), jnp.int32)
    for block in range(6):
        pair_ref[block : block + 1, 0:64] = cell_list_ref[block : block + 1, :]
    lists = pair_ref[...]
    turned = turn(lists)
    for group in range(3):
        index = wide(lists[2 * group : 2 * group + 1] + turned[2 * group + 1 : 2 * group + 2])
        low, high = index[:6] & 127, index[:6] >> 7
        edges = jnp.zeros((6, LANES), jnp.int32)
        shares = jnp.zeros((6, LANES), jnp.float32)
        for block in range(BLOCKS):
            columns = slice(block * LANES, (block + 1) * LANES)
            here = high == block
            edges = jnp.where(here, pick(cells_ref[:, columns], low), edges)
            shares = jnp.where(here, pick(share_ref[:, columns], low), shares)
        names = (edges - LOCAL).astype(jnp.float32)
        tables = (halves(names, turn(shares)), halves(turn(names), shares))
        sums = [jnp.zeros((8, LANES), jnp.float32) for _ in range(2)]
        for side in range(6):
            index, share = wide(edges[side : side + 1]), wide(shares[side : side + 1])
            low, high = index & 127, index >> 7
            for part in range(3):
                weight = jnp.where(high == spot + 8 * part, share, 0.0)
                for level in range(2):
                    got = pick(table_ref[level * 3 + part], low)
                    sums[level] = sums[level] + weight * (got * got)
        sums = [total(part) for part in sums]
        parts = (halves(sums[0], turn(sums[1])), halves(turn(sums[0]), sums[1]))
        for half in range(2):
            block = 2 * group + half
            way, place = WAY * (block // 3), block % 3
            sent_ref[way + 2 + place, 0:6, :] = tables[half]
            row = 6 + place % 2
            sent_ref[way + place // 2, row : row + 1, :] = parts[half]


def local_kernel(
    table_ref, near_ref, weight_ref, cells_ref, share_ref, sums_ref, energy_ref,
):
    spot = sublanes()
    table = split(table_ref[...].reshape(18 * 8, LANES), 1)
    counts = counting()

    def edges(step, carry):
        columns = pl.ds(pl.multiple_of(step * SPAN, SPAN), SPAN)
        sums = [[jnp.zeros((8, LANES), jnp.float32) for _ in range(6)] for _ in range(2)]
        for side in range(10):
            index, weight = near_ref[side : side + 1, columns], weight_ref[side : side + 1, columns]
            if side < PRODUCTS:
                ones = ones_at(index, counts)
                got = product(table, jnp.concatenate([ones, ones], axis=0))
            for half in range(2):
                part_of = slice(half * LANES, (half + 1) * LANES)
                low, high = wide(index[:, part_of]) & 127, wide(index[:, part_of]) >> 7
                share = wide(weight[:, part_of])
                for part in range(3):
                    here = jnp.where(high == spot + 8 * part, share, 0.0)
                    for field in range(6):
                        tile = field * 3 + part
                        if side < PRODUCTS:
                            values = got[tile * 8 : tile * 8 + 8, part_of]
                        else:
                            values = pick(table_ref[tile], low)
                        sums[half][field] = sums[half][field] + here * values
        for half in range(2):
            for field in range(6):
                sums_ref[step * 2 + half, field] = sums[half][field]
        return carry

    lax.fori_loop(0, ROWS // 2, edges, 0, unroll=True)

    def cells(step, carry):
        columns = pl.ds(pl.multiple_of(step * LANES, LANES), LANES)
        sums = [jnp.zeros((8, LANES), jnp.float32) for _ in range(2)]
        for side in range(6):
            index = wide(cells_ref[side : side + 1, columns])
            share = wide(share_ref[side : side + 1, columns])
            low, high = index & 127, index >> 7
            for part in range(3):
                here = jnp.where(high == spot + 8 * part, share, 0.0)
                for level in range(2):
                    got = pick(table_ref[level * 3 + part], low)
                    sums[level] = sums[level] + here * (got * got)
        for level in range(2):
            energy_ref[step, level] = sums[level]
        return carry

    lax.fori_loop(0, BLOCKS, cells, 0, unroll=4)


def finish_kernel(
    core_ref, own_ref, around_ref, sums_ref, energy_sums_ref, near_ref, weight_ref, cells_ref, share_ref,
    ends_ref, inverse_ref, vort_ref, wind_ref, speed_ref, tendency_ref, tangent_ref, energy_ref,
    halo_ref, cell_ref,
):
    core = core_ref[0]
    first = jnp.full((8, LANES), core, jnp.int32) == 0
    spot = sublanes()

    def rows_at(way, tile, rows, place):
        chip, part = place // 2, place % 2
        side = 0 if chip < 0 else 1
        if chip == 0:
            return own_ref[part, way * WAY + tile, rows, :]
        if abs(chip) == 1:
            at = NEAR + part * WAY + tile
        elif abs(chip) == 2 and tile < 2:
            at = MIDDLE + part * 2 + tile
        elif abs(chip) == 2:
            assert part == 1 - side and tile >= 4
            at = MIDDLE + tile
        else:
            assert abs(chip) == 3 and tile < 2
            at = FAR + part * 2 + tile
        return around_ref[side, at, rows, :]

    def rows_of(distance, way, tile, start, stop):
        rows = slice(start, stop)
        on_first = rows_at(way, tile, rows, distance)
        on_second = rows_at(way, tile, rows, distance + 1)
        return jnp.where(first[: stop - start], on_first, on_second)

    for field in range(6):
        halo_ref[field] = jnp.zeros((8, LANES), jnp.float32)
    for block in range(6):
        away, way, place = -OFF[block], block // 3, block % 3
        mass = rows_of(away, way, 2 + place, 6, 8)
        for level in range(2):
            row = slice(block, block + 1)
            halo_ref[level, row, :] = rows_of(away, way, level, block, block + 1)
            halo_ref[2 + level, row, :] = mass[level : level + 1]
            at = level * 3 + place
            halo_ref[4 + level, row, :] = rows_of(away, way, 5, at, at + 1)

    squares = [halo_ref[level] * halo_ref[level] for level in range(2)]
    for step in range(BLOCKS):
        columns = slice(step * LANES, (step + 1) * LANES)
        sums = [energy_sums_ref[step, level] for level in range(2)]
        for side in range(6):
            index = wide(cells_ref[side : side + 1, columns])
            share = wide(share_ref[side : side + 1, columns])
            low, high = index & 127, index >> 7
            here = jnp.where(high == spot + ROWS, share, 0.0)
            for level in range(2):
                sums[level] = sums[level] + here * pick(squares[level], low)
        for level in range(2):
            row = total(sums[level])
            energy_ref[level : level + 1, columns] = row
            cell_ref[level, step : step + 1, :] = row

    for level in range(2):
        cell_ref[2 + level] = jnp.zeros((8, LANES), jnp.float32)
    for group in range(3):
        tables, names, parts = [], [], []
        for half in range(2):
            block = 2 * group + half
            away, way, place = -OFF[block], block // 3, block % 3
            for level in range(2):
                table = jnp.zeros((8, LANES), jnp.float32)
                for sender in range(6):
                    table = jnp.where(spot == sender, rows_of(away - OFF[sender], 0, level, 0, 8), table)
                tables.append(table * table)
            names.append(rows_of(away, way, 2 + place, 0, 8))
            row = 6 + place % 2
            parts.append(rows_of(away, way, place // 2, row, row + 1))
        indices = halves(names[0], turn(names[1])).astype(jnp.int32)
        shares = halves(turn(names[0]), names[1])
        parts = (halves(parts[0], turn(parts[1])), halves(turn(parts[0]), parts[1]))
        sums = [jnp.zeros((8, LANES), jnp.float32) for _ in range(2)]
        for side in range(6):
            index, share = wide(indices[side : side + 1]), wide(shares[side : side + 1])
            low, high = index & 127, index >> 7
            here = jnp.where(high == spot, share, 0.0)
            for level in range(2):
                got = halves(pick(tables[level], low), pick(tables[2 + level], low))
                sums[level] = sums[level] + here * got
        for level in range(2):
            cell_ref[2 + level, group : group + 1, :] = total(sums[level]) + parts[level]

    halo = split(halo_ref[...].reshape(6 * 8, LANES), 0)
    counts = counting()

    def edges(step, carry):
        columns = pl.ds(pl.multiple_of(step * SPAN, SPAN), SPAN)
        sums = [[sums_ref[step * 2 + half, field] for field in range(6)] for half in range(2)]
        for side in range(10):
            index, weight = near_ref[side : side + 1, columns], weight_ref[side : side + 1, columns]
            got = product(halo, ones_at(index, counts))
            got = got[:48] + got[48:]
            for half in range(2):
                part_of = slice(half * LANES, (half + 1) * LANES)
                high = wide(index[:, part_of]) >> 7
                here = jnp.where(high == spot + ROWS, wide(weight[:, part_of]), 0.0)
                for field in range(6):
                    values = got[field * 8 : field * 8 + 8, part_of]
                    sums[half][field] = sums[half][field] + here * values
        for half in range(2):
            block = step * 2 + half
            columns = pl.ds(pl.multiple_of(block * LANES, LANES), LANES)
            slopes = [jnp.zeros((8, LANES), jnp.float32) for _ in range(2)]
            for side in range(2):
                sign = 1.0 if side == 1 else -1.0
                index = wide(ends_ref[side : side + 1, columns])
                low, high = index & 127, index >> 7
                for part in range(2):
                    here = high == spot + BLOCKS * part
                    for level in range(2):
                        got = jnp.where(here, pick(cell_ref[2 * part + level], low), 0.0)
                        slopes[level] = slopes[level] + sign * got
            inverse = wide(inverse_ref[:, columns])
            row, tile = block % 8, block // 8
            below = around_ref[0, EDGE + core * 3 + tile, pl.ds(row, 1), :]
            above = around_ref[1, EDGE + core * 3 + tile, pl.ds(row, 1), :]
            speeds = [speed_ref[level : level + 1, columns] for level in range(2)]
            risers = [speeds[1] - below, above - speeds[0]]
            for level in range(2):
                vort = wide(vort_ref[level : level + 1, columns])
                flux = 0.5 * (vort * sums[half][2 + level] + sums[half][4 + level])
                result = total(flux - slopes[level] * inverse)
                advect = -0.5 * wind_ref[level : level + 1, columns] * risers[level]
                tendency_ref[level : level + 1, columns] = result + advect
                tangent_ref[level : level + 1, columns] = total(sums[half][level])
        return carry

    lax.fori_loop(0, ROWS // 2, edges, 0, unroll=True)


VMEM = pl.BlockSpec(memory_space=pltpu.VMEM)


def body(
    velocity,
    thickness,
    vorticity,
    vertical_wind,
    weights_on_edge,
    edges_on_edge,
    edges_on_cell,
    cells_on_edge,
    energy_weight,
    inverse_distance,
    edge_halo_list,
    edge_halo_count,
    cell_halo_list,
    cell_halo_count,
):
    del edge_halo_count, cell_halo_count
    f32 = jnp.float32
    core = lax.axis_index("core")
    params = pltpu.CompilerParams(vmem_limit_bytes=24 << 20)
    inputs = (
        velocity, thickness, vorticity, edge_halo_list, cell_halo_list, edges_on_cell, energy_weight
    )
    sent, tables = pl.pallas_call(
        pack_kernel,
        out_shape=(
            jax.ShapeDtypeStruct((TILES, 8, LANES), f32),
            jax.ShapeDtypeStruct((18, 8, LANES), f32),
        ),
        in_specs=[pl.BlockSpec(memory_space=pltpu.HBM)] * 7,
        out_specs=(VMEM, VMEM),
        scratch_shapes=[pltpu.VMEM(x.shape, x.dtype) for x in inputs]
        + [pltpu.VMEM((8, LANES), jnp.int32), pltpu.SemaphoreType.DMA((7,))],
        compiler_params=pltpu.CompilerParams(vmem_limit_bytes=60 << 20),
        name="pack",
    )(*inputs)

    mesh_axes = ("x", "z", "core")
    own = lax.all_gather(sent, "core")
    even = core == 0
    near = jnp.where(even, own[:, :WAY], own[:, WAY:RIM])
    rims = jnp.where(even, own[:, RIM + 3 :], own[:, RIM : RIM + 3])
    chips = lax.axis_size("x") * lax.axis_size("z")

    def apart(block, distance):
        right = [(2 * c, 2 * ((c + distance) % chips)) for c in range(chips)]
        left = [(2 * c + 1, 2 * ((c - distance) % chips) + 1) for c in range(chips)]
        return lax.ppermute(block, mesh_axes, right + left)

    groups = lax.axis_size("lev")
    up = [(i, i + 1) for i in range(groups - 1)]
    down = [(groups + i + 1, groups + i) for i in range(groups - 1)]
    speeds = near[:, :2].reshape(4, 8, LANES)
    rest = jnp.where(even, near[1, 4:], near[0, 4:])
    spare = near[1]
    arrived = [
        apart(near, 1).reshape(12, 8, LANES),
        apart(jnp.concatenate([speeds, rest, spare[:1]], axis=0), 2),
        apart(jnp.concatenate([speeds, spare[:4]], axis=0), 3),
        lax.ppermute(rims, ("core", "lev"), up + down).reshape(6, 8, LANES),
    ]
    arrived = jnp.concatenate(arrived, axis=0)
    sums, energy_sums = pl.pallas_call(
        local_kernel,
        out_shape=(
            jax.ShapeDtypeStruct((ROWS, 6, 8, LANES), f32),
            jax.ShapeDtypeStruct((BLOCKS, 2, 8, LANES), f32),
        ),
        in_specs=[VMEM] * 5,
        out_specs=(VMEM, VMEM),
        compiler_params=params,
        cost_estimate=pl.CostEstimate(flops=20_000_000, bytes_accessed=1_000_000, transcendentals=0),
        name="local",
    )(tables, edges_on_edge, weights_on_edge, edges_on_cell, energy_weight)
    around = lax.all_gather(arrived, "core")
    return pl.pallas_call(
        finish_kernel,
        out_shape=(
            jax.ShapeDtypeStruct(velocity.shape, f32),
            jax.ShapeDtypeStruct(velocity.shape, f32),
            jax.ShapeDtypeStruct((velocity.shape[0], edges_on_cell.shape[1]), f32),
        ),
        in_specs=[pl.BlockSpec(memory_space=pltpu.SMEM)] + [VMEM] * 13,
        out_specs=(VMEM, VMEM, VMEM),
        scratch_shapes=[pltpu.VMEM((6, 8, LANES), f32), pltpu.VMEM((4, 8, LANES), f32)],
        compiler_params=params,
        name="finish",
    )(
        core.astype(jnp.int32).reshape(1), own, around, sums, energy_sums, edges_on_edge, weights_on_edge,
        edges_on_cell, energy_weight, cells_on_edge, inverse_distance.reshape(1, -1), vorticity,
        vertical_wind, velocity,
    )


def solution(mesh):
    fine = Mesh(mesh.devices.reshape(4, 12, 2, 8), ("x", "z", "core", "lev"))
    parts = ("x", "z", "core")
    in_specs = (
        P("lev", parts),
        P("lev", parts),
        P("lev", parts),
        P("lev", parts),
        P(None, parts),
        P(None, parts),
        P(None, parts),
        P(None, parts),
        P(None, parts),
        P(parts),
        P(parts, None),
        P(parts),
        P(parts, None),
        P(parts),
    )
    out_specs = (P("lev", parts), P("lev", parts), P("lev", parts))
    return jax.shard_map(body, mesh=fine, in_specs=in_specs, out_specs=out_specs, check_vma=False)
```

```python
import jax
import jax.numpy as jnp
from jax import lax
from jax.experimental import pallas as pl
from jax.experimental.pallas import tpu as pltpu
from jax.sharding import Mesh, PartitionSpec as P

OFF = (1, 2, 3, -1, -2, -3)
LANES = 128
ROWS = 24
LOCAL = ROWS * LANES
BLOCKS = 8

WAY = 6
RIM = 2 * WAY
TILES = RIM + 6
NEAR, MIDDLE, FAR, EDGE = 0, 12, 19, 27


def pick(table, low):
    return jnp.take_along_axis(table, low, axis=1, mode="promise_in_bounds")


def wide(row):
    return jnp.broadcast_to(row, (8, LANES))


def sublanes():
    return lax.broadcasted_iota(jnp.int32, (8, LANES), 0)


def total(tile):
    return jnp.sum(tile, axis=0, keepdims=True)


SPAN = 2 * LANES


def split(table, axis):
    coarse = table.astype(jnp.bfloat16)
    fine = (table - coarse.astype(jnp.float32)).astype(jnp.bfloat16)
    return jnp.concatenate([coarse, fine], axis=axis)


def ones_at(index, counts):
    low = (index & 127).astype(jnp.float32).astype(jnp.bfloat16)
    here = counts == jnp.broadcast_to(low, (LANES, SPAN))
    return jnp.where(here, jnp.bfloat16(1), jnp.bfloat16(0))


def product(table, ones):
    return jnp.dot(table, ones, preferred_element_type=jnp.float32)


def counting():
    return lax.broadcasted_iota(jnp.int32, (LANES, SPAN), 0).astype(jnp.float32).astype(jnp.bfloat16)


def halves(left, right):
    lane = lax.broadcasted_iota(jnp.int32, left.shape, 1)
    return jnp.where(lane < 64, left, right)


def turn(tile):
    return pltpu.roll(tile, 64, 1)


def pack_kernel(
    speed_hbm, height_hbm, vort_hbm, edge_list_hbm, cell_list_hbm, cells_hbm, share_hbm,
    sent_ref, table_ref,
    speed_ref, height_ref, vort_ref, edge_list_ref, cell_list_ref, cells_ref, share_ref, pair_ref, done,
):
    pairs = (
        (speed_hbm, speed_ref), (height_hbm, height_ref), (vort_hbm, vort_ref), (edge_list_hbm, edge_list_ref),
        (cell_list_hbm, cell_list_ref), (cells_hbm, cells_ref), (share_hbm, share_ref),
    )
    copies = [pltpu.make_async_copy(src, dst, done.at[i]) for i, (src, dst) in enumerate(pairs)]
    for copy in copies:
        copy.start()
    for copy in copies:
        copy.wait()
    for level in range(2):
        for row in range(ROWS):
            tile, place = level * 3 + row // 8, slice(row % 8, row % 8 + 1)
            columns = slice(row * LANES, (row + 1) * LANES)
            table_ref[tile, place, :] = speed_ref[level : level + 1, columns]
            table_ref[6 + tile, place, :] = height_ref[level : level + 1, columns]
            table_ref[12 + tile, place, :] = vort_ref[level : level + 1, columns]
    for tile in range(6):
        speed = table_ref[tile]
        mass = speed * table_ref[6 + tile]
        table_ref[6 + tile] = mass
        table_ref[12 + tile] = mass * table_ref[12 + tile]
        sent_ref[RIM + tile] = speed
    for way in range(2):
        for tile in (0, 1, 5):
            sent_ref[way * WAY + tile] = jnp.zeros((8, LANES), jnp.float32)
    spot = sublanes()
    for block in range(6):
        index = wide(edge_list_ref[block : block + 1, :])
        low, high = index & 127, index >> 7
        way, place = WAY * (block // 3), block % 3
        for field in range(6):
            found = jnp.zeros((8, LANES), jnp.float32)
            for part in range(3):
                got = pick(table_ref[field * 3 + part], low)
                found = jnp.where(high == spot + 8 * part, got, found)
            row, level = total(found), field % 2
            if field < 2:
                sent_ref[level, block : block + 1, :] = row
                sent_ref[WAY + level, block : block + 1, :] = row
            elif field < 4:
                sent_ref[way + 2 + place, 6 + level : 7 + level, :] = row
            else:
                sent_ref[way + 5, level * 3 + place : level * 3 + place + 1, :] = row
    pair_ref[...] = jnp.zeros((8, LANES), jnp.int32)
    for block in range(6):
        pair_ref[block : block + 1, 0:64] = cell_list_ref[block : block + 1, :]
    lists = pair_ref[...]
    turned = turn(lists)
    for group in range(3):
        index = wide(lists[2 * group : 2 * group + 1] + turned[2 * group + 1 : 2 * group + 2])
        low, high = index[:6] & 127, index[:6] >> 7
        edges = jnp.zeros((6, LANES), jnp.int32)
        shares = jnp.zeros((6, LANES), jnp.float32)
        for block in range(BLOCKS):
            columns = slice(block * LANES, (block + 1) * LANES)
            here = high == block
            edges = jnp.where(here, pick(cells_ref[:, columns], low), edges)
            shares = jnp.where(here, pick(share_ref[:, columns], low), shares)
        names = (edges - LOCAL).astype(jnp.float32)
        tables = (halves(names, turn(shares)), halves(turn(names), shares))
        sums = [jnp.zeros((8, LANES), jnp.float32) for _ in range(2)]
        for side in range(6):
            index, share = wide(edges[side : side + 1]), wide(shares[side : side + 1])
            low, high = index & 127, index >> 7
            for part in range(3):
                weight = jnp.where(high == spot + 8 * part, share, 0.0)
                for level in range(2):
                    got = pick(table_ref[level * 3 + part], low)
                    sums[level] = sums[level] + weight * (got * got)
        sums = [total(part) for part in sums]
        parts = (halves(sums[0], turn(sums[1])), halves(turn(sums[0]), sums[1]))
        for half in range(2):
            block = 2 * group + half
            way, place = WAY * (block // 3), block % 3
            sent_ref[way + 2 + place, 0:6, :] = tables[half]
            row = 6 + place % 2
            sent_ref[way + place // 2, row : row + 1, :] = parts[half]


def local_kernel(
    table_ref, near_ref, weight_ref, cells_ref, share_ref, sums_ref, energy_ref,
):
    spot = sublanes()
    table = split(table_ref[...].reshape(18 * 8, LANES), 1)
    counts = counting()

    def edges(step, carry):
        columns = pl.ds(pl.multiple_of(step * SPAN, SPAN), SPAN)
        sums = [[jnp.zeros((8, LANES), jnp.float32) for _ in range(6)] for _ in range(2)]
        for side in range(10):
            index, weight = near_ref[side : side + 1, columns], weight_ref[side : side + 1, columns]
            ones = ones_at(index, counts)
            got = product(table, jnp.concatenate([ones, ones], axis=0))
            for half in range(2):
                part_of = slice(half * LANES, (half + 1) * LANES)
                high = wide(index[:, part_of]) >> 7
                share = wide(weight[:, part_of])
                for part in range(3):
                    here = jnp.where(high == spot + 8 * part, share, 0.0)
                    for field in range(6):
                        row = (field * 3 + part) * 8
                        sums[half][field] = sums[half][field] + here * got[row : row + 8, part_of]
        for half in range(2):
            for field in range(6):
                sums_ref[step * 2 + half, field] = sums[half][field]
        return carry

    lax.fori_loop(0, ROWS // 2, edges, 0, unroll=True)

    def cells(step, carry):
        columns = pl.ds(pl.multiple_of(step * LANES, LANES), LANES)
        sums = [jnp.zeros((8, LANES), jnp.float32) for _ in range(2)]
        for side in range(6):
            index = wide(cells_ref[side : side + 1, columns])
            share = wide(share_ref[side : side + 1, columns])
            low, high = index & 127, index >> 7
            for part in range(3):
                here = jnp.where(high == spot + 8 * part, share, 0.0)
                for level in range(2):
                    got = pick(table_ref[level * 3 + part], low)
                    sums[level] = sums[level] + here * (got * got)
        for level in range(2):
            energy_ref[step, level] = sums[level]
        return carry

    lax.fori_loop(0, BLOCKS, cells, 0, unroll=True)


def finish_kernel(
    core_ref, own_ref, around_ref, sums_ref, energy_sums_ref, near_ref, weight_ref, cells_ref, share_ref,
    ends_ref, inverse_ref, vort_ref, wind_ref, speed_ref, tendency_ref, tangent_ref, energy_ref,
    halo_ref, cell_ref,
):
    core = core_ref[0]
    first = jnp.full((8, LANES), core, jnp.int32) == 0
    spot = sublanes()

    def rows_at(way, tile, rows, place):
        chip, part = place // 2, place % 2
        side = 0 if chip < 0 else 1
        if chip == 0:
            return own_ref[part, way * WAY + tile, rows, :]
        if abs(chip) == 1:
            at = NEAR + part * WAY + tile
        elif abs(chip) == 2 and tile < 2:
            at = MIDDLE + part * 2 + tile
        elif abs(chip) == 2:
            assert part == 1 - side and tile >= 4
            at = MIDDLE + tile
        else:
            assert abs(chip) == 3 and tile < 2
            at = FAR + part * 2 + tile
        return around_ref[side, at, rows, :]

    def rows_of(distance, way, tile, start, stop):
        rows = slice(start, stop)
        on_first = rows_at(way, tile, rows, distance)
        on_second = rows_at(way, tile, rows, distance + 1)
        return jnp.where(first[: stop - start], on_first, on_second)

    for field in range(6):
        halo_ref[field] = jnp.zeros((8, LANES), jnp.float32)
    for block in range(6):
        away, way, place = -OFF[block], block // 3, block % 3
        mass = rows_of(away, way, 2 + place, 6, 8)
        for level in range(2):
            row = slice(block, block + 1)
            halo_ref[level, row, :] = rows_of(away, way, level, block, block + 1)
            halo_ref[2 + level, row, :] = mass[level : level + 1]
            at = level * 3 + place
            halo_ref[4 + level, row, :] = rows_of(away, way, 5, at, at + 1)

    squares = [halo_ref[level] * halo_ref[level] for level in range(2)]
    for step in range(BLOCKS):
        columns = slice(step * LANES, (step + 1) * LANES)
        sums = [energy_sums_ref[step, level] for level in range(2)]
        for side in range(6):
            index = wide(cells_ref[side : side + 1, columns])
            share = wide(share_ref[side : side + 1, columns])
            low, high = index & 127, index >> 7
            here = jnp.where(high == spot + ROWS, share, 0.0)
            for level in range(2):
                sums[level] = sums[level] + here * pick(squares[level], low)
        for level in range(2):
            row = total(sums[level])
            energy_ref[level : level + 1, columns] = row
            cell_ref[level, step : step + 1, :] = row

    for level in range(2):
        cell_ref[2 + level] = jnp.zeros((8, LANES), jnp.float32)
    for group in range(3):
        tables, names, parts = [], [], []
        for half in range(2):
            block = 2 * group + half
            away, way, place = -OFF[block], block // 3, block % 3
            for level in range(2):
                table = jnp.zeros((8, LANES), jnp.float32)
                for sender in range(6):
                    table = jnp.where(spot == sender, rows_of(away - OFF[sender], 0, level, 0, 8), table)
                tables.append(table * table)
            names.append(rows_of(away, way, 2 + place, 0, 8))
            row = 6 + place % 2
            parts.append(rows_of(away, way, place // 2, row, row + 1))
        indices = halves(names[0], turn(names[1])).astype(jnp.int32)
        shares = halves(turn(names[0]), names[1])
        parts = (halves(parts[0], turn(parts[1])), halves(turn(parts[0]), parts[1]))
        sums = [jnp.zeros((8, LANES), jnp.float32) for _ in range(2)]
        for side in range(6):
            index, share = wide(indices[side : side + 1]), wide(shares[side : side + 1])
            low, high = index & 127, index >> 7
            here = jnp.where(high == spot, share, 0.0)
            for level in range(2):
                got = halves(pick(tables[level], low), pick(tables[2 + level], low))
                sums[level] = sums[level] + here * got
        for level in range(2):
            cell_ref[2 + level, group : group + 1, :] = total(sums[level]) + parts[level]

    halo = split(halo_ref[...].reshape(6 * 8, LANES), 0)
    counts = counting()

    def edges(step, carry):
        columns = pl.ds(pl.multiple_of(step * SPAN, SPAN), SPAN)
        sums = [[sums_ref[step * 2 + half, field] for field in range(6)] for half in range(2)]
        for side in range(10):
            index, weight = near_ref[side : side + 1, columns], weight_ref[side : side + 1, columns]
            got = product(halo, ones_at(index, counts))
            got = got[:48] + got[48:]
            for half in range(2):
                part_of = slice(half * LANES, (half + 1) * LANES)
                high = wide(index[:, part_of]) >> 7
                here = jnp.where(high == spot + ROWS, wide(weight[:, part_of]), 0.0)
                for field in range(6):
                    values = got[field * 8 : field * 8 + 8, part_of]
                    sums[half][field] = sums[half][field] + here * values
        for half in range(2):
            block = step * 2 + half
            columns = pl.ds(pl.multiple_of(block * LANES, LANES), LANES)
            slopes = [jnp.zeros((8, LANES), jnp.float32) for _ in range(2)]
            for side in range(2):
                sign = 1.0 if side == 1 else -1.0
                index = wide(ends_ref[side : side + 1, columns])
                low, high = index & 127, index >> 7
                for part in range(2):
                    here = high == spot + BLOCKS * part
                    for level in range(2):
                        got = jnp.where(here, pick(cell_ref[2 * part + level], low), 0.0)
                        slopes[level] = slopes[level] + sign * got
            inverse = wide(inverse_ref[:, columns])
            row, tile = block % 8, block // 8
            below = around_ref[0, EDGE + core * 3 + tile, pl.ds(row, 1), :]
            above = around_ref[1, EDGE + core * 3 + tile, pl.ds(row, 1), :]
            speeds = [speed_ref[level : level + 1, columns] for level in range(2)]
            risers = [speeds[1] - below, above - speeds[0]]
            for level in range(2):
                vort = wide(vort_ref[level : level + 1, columns])
                flux = 0.5 * (vort * sums[half][2 + level] + sums[half][4 + level])
                result = total(flux - slopes[level] * inverse)
                advect = -0.5 * wind_ref[level : level + 1, columns] * risers[level]
                tendency_ref[level : level + 1, columns] = result + advect
                tangent_ref[level : level + 1, columns] = total(sums[half][level])
        return carry

    lax.fori_loop(0, ROWS // 2, edges, 0, unroll=True)


VMEM = pl.BlockSpec(memory_space=pltpu.VMEM)


def body(
    velocity,
    thickness,
    vorticity,
    vertical_wind,
    weights_on_edge,
    edges_on_edge,
    edges_on_cell,
    cells_on_edge,
    energy_weight,
    inverse_distance,
    edge_halo_list,
    edge_halo_count,
    cell_halo_list,
    cell_halo_count,
):
    del edge_halo_count, cell_halo_count
    f32 = jnp.float32
    core = lax.axis_index("core")
    params = pltpu.CompilerParams(vmem_limit_bytes=24 << 20)
    inputs = (
        velocity, thickness, vorticity, edge_halo_list, cell_halo_list, edges_on_cell, energy_weight
    )
    sent, tables = pl.pallas_call(
        pack_kernel,
        out_shape=(
            jax.ShapeDtypeStruct((TILES, 8, LANES), f32),
            jax.ShapeDtypeStruct((18, 8, LANES), f32),
        ),
        in_specs=[pl.BlockSpec(memory_space=pltpu.HBM)] * 7,
        out_specs=(VMEM, VMEM),
        scratch_shapes=[pltpu.VMEM(x.shape, x.dtype) for x in inputs]
        + [pltpu.VMEM((8, LANES), jnp.int32), pltpu.SemaphoreType.DMA((7,))],
        compiler_params=params,
        name="pack",
    )(*(pltpu.with_memory_space_constraint(x, pltpu.HBM) for x in inputs))

    mesh_axes = ("x", "z", "core")
    own = lax.all_gather(sent, "core")
    even = core == 0
    near = jnp.where(even, own[:, :WAY], own[:, WAY:RIM])
    rims = jnp.where(even, own[:, RIM + 3 :], own[:, RIM : RIM + 3])
    chips = lax.axis_size("x") * lax.axis_size("z")

    def apart(block, distance):
        right = [(2 * c, 2 * ((c + distance) % chips)) for c in range(chips)]
        left = [(2 * c + 1, 2 * ((c - distance) % chips) + 1) for c in range(chips)]
        return lax.ppermute(block, mesh_axes, right + left)

    groups = lax.axis_size("lev")
    up = [(i, i + 1) for i in range(groups - 1)]
    down = [(groups + i + 1, groups + i) for i in range(groups - 1)]
    speeds = near[:, :2].reshape(4, 8, LANES)
    rest = jnp.where(even, near[1, 4:], near[0, 4:])
    spare = near[1]
    arrived = [
        apart(near, 1).reshape(12, 8, LANES),
        apart(jnp.concatenate([speeds, rest, spare[:1]], axis=0), 2),
        apart(jnp.concatenate([speeds, spare[:4]], axis=0), 3),
        lax.ppermute(rims, ("core", "lev"), up + down).reshape(6, 8, LANES),
    ]
    arrived = jnp.concatenate(arrived, axis=0)
    sums, energy_sums = pl.pallas_call(
        local_kernel,
        out_shape=(
            jax.ShapeDtypeStruct((ROWS, 6, 8, LANES), f32),
            jax.ShapeDtypeStruct((BLOCKS, 2, 8, LANES), f32),
        ),
        in_specs=[VMEM] * 5,
        out_specs=(VMEM, VMEM),
        compiler_params=params,
        cost_estimate=pl.CostEstimate(flops=20_000_000, bytes_accessed=1_000_000, transcendentals=0),
        name="local",
    )(tables, edges_on_edge, weights_on_edge, edges_on_cell, energy_weight)
    around = lax.all_gather(arrived, "core")
    return pl.pallas_call(
        finish_kernel,
        out_shape=(
            jax.ShapeDtypeStruct(velocity.shape, f32),
            jax.ShapeDtypeStruct(velocity.shape, f32),
            jax.ShapeDtypeStruct((velocity.shape[0], edges_on_cell.shape[1]), f32),
        ),
        in_specs=[pl.BlockSpec(memory_space=pltpu.SMEM)] + [VMEM] * 13,
        out_specs=(VMEM, VMEM, VMEM),
        scratch_shapes=[pltpu.VMEM((6, 8, LANES), f32), pltpu.VMEM((4, 8, LANES), f32)],
        compiler_params=params,
        name="finish",
    )(
        core.astype(jnp.int32).reshape(1), own, around, sums, energy_sums, edges_on_edge, weights_on_edge,
        edges_on_cell, energy_weight, cells_on_edge, inverse_distance.reshape(1, -1), vorticity,
        vertical_wind, velocity,
    )


def solution(mesh):
    fine = Mesh(mesh.devices.reshape(4, 12, 2, 8), ("x", "z", "core", "lev"))
    parts = ("x", "z", "core")
    in_specs = (
        P("lev", parts),
        P("lev", parts),
        P("lev", parts),
        P("lev", parts),
        P(None, parts),
        P(None, parts),
        P(None, parts),
        P(None, parts),
        P(None, parts),
        P(parts),
        P(parts, None),
        P(parts),
        P(parts, None),
        P(parts),
    )
    out_specs = (P("lev", parts), P("lev", parts), P("lev", parts))
    return jax.shard_map(body, mesh=fine, in_specs=in_specs, out_specs=out_specs, check_vma=False)
```

```python
import jax
import jax.numpy as jnp
from jax import lax
from jax.experimental import pallas as pl
from jax.experimental.pallas import tpu as pltpu
from jax.sharding import Mesh, PartitionSpec as P

OFF = (1, 2, 3, -1, -2, -3)
LANES = 128
ROWS = 24
LOCAL = ROWS * LANES
BLOCKS = 8

WAY = 6
RIM = 2 * WAY
TILES = RIM + 6
EARLY = 4
NEAR, MIDDLE, FAR, EDGE = 0, 12, 20, 27


def pick(table, low):
    return jnp.take_along_axis(table, low, axis=1, mode="promise_in_bounds")


def wide(row):
    return jnp.broadcast_to(row, (8, LANES))


def sublanes():
    return lax.broadcasted_iota(jnp.int32, (8, LANES), 0)


def total(tile):
    return jnp.sum(tile, axis=0, keepdims=True)


SPAN = 2 * LANES


def split(table, axis):
    coarse = table.astype(jnp.bfloat16)
    fine = (table - coarse.astype(jnp.float32)).astype(jnp.bfloat16)
    return jnp.concatenate([coarse, fine], axis=axis)


def ones_at(index, counts):
    low = (index & 127).astype(jnp.float32).astype(jnp.bfloat16)
    here = counts == jnp.broadcast_to(low, (LANES, SPAN))
    return jnp.where(here, jnp.bfloat16(1), jnp.bfloat16(0))


def product(table, ones):
    return jnp.dot(table, ones, preferred_element_type=jnp.float32)


def counting():
    return lax.broadcasted_iota(jnp.int32, (LANES, SPAN), 0).astype(jnp.float32).astype(jnp.bfloat16)


def halves(left, right):
    lane = lax.broadcasted_iota(jnp.int32, left.shape, 1)
    return jnp.where(lane < 64, left, right)


def turn(tile):
    return pltpu.roll(tile, 64, 1)


def pack_kernel(
    speed_hbm, height_hbm, vort_hbm, edge_list_hbm, cell_list_hbm, cells_hbm, share_hbm,
    sent_ref, table_ref,
    speed_ref, height_ref, vort_ref, edge_list_ref, cell_list_ref, cells_ref, share_ref, pair_ref, done,
):
    pairs = (
        (speed_hbm, speed_ref), (height_hbm, height_ref), (vort_hbm, vort_ref), (edge_list_hbm, edge_list_ref),
        (cell_list_hbm, cell_list_ref), (cells_hbm, cells_ref), (share_hbm, share_ref),
    )
    copies = [pltpu.make_async_copy(src, dst, done.at[i]) for i, (src, dst) in enumerate(pairs)]
    for copy in copies:
        copy.start()
    for copy in copies:
        copy.wait()
    for level in range(2):
        for row in range(ROWS):
            tile, place = level * 3 + row // 8, slice(row % 8, row % 8 + 1)
            columns = slice(row * LANES, (row + 1) * LANES)
            table_ref[tile, place, :] = speed_ref[level : level + 1, columns]
            table_ref[6 + tile, place, :] = height_ref[level : level + 1, columns]
            table_ref[12 + tile, place, :] = vort_ref[level : level + 1, columns]
    for tile in range(6):
        speed = table_ref[tile]
        mass = speed * table_ref[6 + tile]
        table_ref[6 + tile] = mass
        table_ref[12 + tile] = mass * table_ref[12 + tile]
        sent_ref[RIM + tile] = speed
    for way in range(2):
        for tile in (0, 1, 5):
            sent_ref[way * WAY + tile] = jnp.zeros((8, LANES), jnp.float32)
    spot = sublanes()
    for block in range(6):
        index = wide(edge_list_ref[block : block + 1, :])
        low, high = index & 127, index >> 7
        way, place = WAY * (block // 3), block % 3
        for field in range(6):
            found = jnp.zeros((8, LANES), jnp.float32)
            for part in range(3):
                got = pick(table_ref[field * 3 + part], low)
                found = jnp.where(high == spot + 8 * part, got, found)
            row, level = total(found), field % 2
            if field < 2:
                sent_ref[level, block : block + 1, :] = row
                sent_ref[WAY + level, block : block + 1, :] = row
            elif field < 4:
                sent_ref[way + 2 + place, 6 + level : 7 + level, :] = row
            else:
                sent_ref[way + 5, level * 3 + place : level * 3 + place + 1, :] = row
    pair_ref[...] = jnp.zeros((8, LANES), jnp.int32)
    for block in range(6):
        pair_ref[block : block + 1, 0:64] = cell_list_ref[block : block + 1, :]
    lists = pair_ref[...]
    turned = turn(lists)
    for group in range(3):
        index = wide(lists[2 * group : 2 * group + 1] + turned[2 * group + 1 : 2 * group + 2])
        low, high = index[:6] & 127, index[:6] >> 7
        edges = jnp.zeros((6, LANES), jnp.int32)
        shares = jnp.zeros((6, LANES), jnp.float32)
        for block in range(BLOCKS):
            columns = slice(block * LANES, (block + 1) * LANES)
            here = high == block
            edges = jnp.where(here, pick(cells_ref[:, columns], low), edges)
            shares = jnp.where(here, pick(share_ref[:, columns], low), shares)
        names = (edges - LOCAL).astype(jnp.float32)
        tables = (halves(names, turn(shares)), halves(turn(names), shares))
        sums = [jnp.zeros((8, LANES), jnp.float32) for _ in range(2)]
        for side in range(6):
            index, share = wide(edges[side : side + 1]), wide(shares[side : side + 1])
            low, high = index & 127, index >> 7
            for part in range(3):
                weight = jnp.where(high == spot + 8 * part, share, 0.0)
                for level in range(2):
                    got = pick(table_ref[level * 3 + part], low)
                    sums[level] = sums[level] + weight * (got * got)
        sums = [total(part) for part in sums]
        parts = (halves(sums[0], turn(sums[1])), halves(turn(sums[0]), sums[1]))
        for half in range(2):
            block = 2 * group + half
            way, place = WAY * (block // 3), block % 3
            sent_ref[way + 2 + place, 0:6, :] = tables[half]
            row = 6 + place % 2
            sent_ref[way + place // 2, row : row + 1, :] = parts[half]


def local_early_kernel(early_ref, table_ref, near_ref, weight_ref, sums_ref):
    @pl.when(early_ref[0] == 1)
    def _():
        local_sums(table_ref, near_ref, weight_ref, sums_ref)


def local_late_kernel(
    early_ref, made_ref, table_ref, near_ref, weight_ref, cells_ref, share_ref, sums_ref, energy_ref,
):
    @pl.when(early_ref[0] == 1)
    def _():
        sums_ref[...] = made_ref[...]
        cell_sums(table_ref, cells_ref, share_ref, energy_ref)

    @pl.when(early_ref[0] == 0)
    def _():
        local_sums(table_ref, near_ref, weight_ref, sums_ref)
        cell_sums(table_ref, cells_ref, share_ref, energy_ref)


def local_sums(table_ref, near_ref, weight_ref, sums_ref):
    spot = sublanes()
    table = split(table_ref[...].reshape(18 * 8, LANES), 1)
    counts = counting()

    def edges(step, carry):
        columns = pl.ds(pl.multiple_of(step * SPAN, SPAN), SPAN)
        sums = [[jnp.zeros((8, LANES), jnp.float32) for _ in range(6)] for _ in range(2)]
        for side in range(10):
            index, weight = near_ref[side : side + 1, columns], weight_ref[side : side + 1, columns]
            ones = ones_at(index, counts)
            got = product(table, jnp.concatenate([ones, ones], axis=0))
            for half in range(2):
                part_of = slice(half * LANES, (half + 1) * LANES)
                high = wide(index[:, part_of]) >> 7
                share = wide(weight[:, part_of])
                for part in range(3):
                    here = jnp.where(high == spot + 8 * part, share, 0.0)
                    for field in range(6):
                        row = (field * 3 + part) * 8
                        sums[half][field] = sums[half][field] + here * got[row : row + 8, part_of]
        for half in range(2):
            for field in range(6):
                sums_ref[step * 2 + half, field] = sums[half][field]
        return carry

    lax.fori_loop(0, ROWS // 2, edges, 0, unroll=True)


def cell_sums(table_ref, cells_ref, share_ref, energy_ref):
    spot = sublanes()

    def cells(step, carry):
        columns = pl.ds(pl.multiple_of(step * LANES, LANES), LANES)
        sums = [jnp.zeros((8, LANES), jnp.float32) for _ in range(2)]
        for side in range(6):
            index = wide(cells_ref[side : side + 1, columns])
            share = wide(share_ref[side : side + 1, columns])
            low, high = index & 127, index >> 7
            for part in range(3):
                here = jnp.where(high == spot + 8 * part, share, 0.0)
                for level in range(2):
                    got = pick(table_ref[level * 3 + part], low)
                    sums[level] = sums[level] + here * (got * got)
        for level in range(2):
            energy_ref[step, level] = sums[level]
        return carry

    lax.fori_loop(0, BLOCKS, cells, 0, unroll=True)


def finish_kernel(
    core_ref, own_ref, around_ref, sums_ref, energy_sums_ref, near_ref, weight_ref, cells_ref, share_ref,
    ends_ref, inverse_ref, vort_ref, wind_ref, speed_ref, tendency_ref, tangent_ref, energy_ref,
    halo_ref, cell_ref,
):
    core = core_ref[0]
    first = jnp.full((8, LANES), core, jnp.int32) == 0
    spot = sublanes()

    def rows_at(way, tile, rows, place):
        chip, part = place // 2, place % 2
        side = 0 if chip < 0 else 1
        if chip == 0:
            return own_ref[part, way * WAY + tile, rows, :]
        if abs(chip) == 1:
            at = NEAR + part * WAY + tile
        elif abs(chip) == 2 and tile < 2:
            at = MIDDLE + part * 2 + tile
        elif abs(chip) == 2:
            assert part == 1 - side and tile >= 4
            at = MIDDLE + tile
        else:
            assert abs(chip) == 3 and tile < 2
            at = FAR + part * 2 + tile
        return around_ref[side, at, rows, :]

    def rows_of(distance, way, tile, start, stop):
        rows = slice(start, stop)
        on_first = rows_at(way, tile, rows, distance)
        on_second = rows_at(way, tile, rows, distance + 1)
        return jnp.where(first[: stop - start], on_first, on_second)

    for field in range(6):
        halo_ref[field] = jnp.zeros((8, LANES), jnp.float32)
    for block in range(6):
        away, way, place = -OFF[block], block // 3, block % 3
        mass = rows_of(away, way, 2 + place, 6, 8)
        for level in range(2):
            row = slice(block, block + 1)
            halo_ref[level, row, :] = rows_of(away, way, level, block, block + 1)
            halo_ref[2 + level, row, :] = mass[level : level + 1]
            at = level * 3 + place
            halo_ref[4 + level, row, :] = rows_of(away, way, 5, at, at + 1)

    squares = [halo_ref[level] * halo_ref[level] for level in range(2)]
    for step in range(BLOCKS):
        columns = slice(step * LANES, (step + 1) * LANES)
        sums = [energy_sums_ref[step, level] for level in range(2)]
        for side in range(6):
            index = wide(cells_ref[side : side + 1, columns])
            share = wide(share_ref[side : side + 1, columns])
            low, high = index & 127, index >> 7
            here = jnp.where(high == spot + ROWS, share, 0.0)
            for level in range(2):
                sums[level] = sums[level] + here * pick(squares[level], low)
        for level in range(2):
            row = total(sums[level])
            energy_ref[level : level + 1, columns] = row
            cell_ref[level, step : step + 1, :] = row

    for level in range(2):
        cell_ref[2 + level] = jnp.zeros((8, LANES), jnp.float32)
    for group in range(3):
        tables, names, parts = [], [], []
        for half in range(2):
            block = 2 * group + half
            away, way, place = -OFF[block], block // 3, block % 3
            for level in range(2):
                table = jnp.zeros((8, LANES), jnp.float32)
                for sender in range(6):
                    table = jnp.where(spot == sender, rows_of(away - OFF[sender], 0, level, 0, 8), table)
                tables.append(table * table)
            names.append(rows_of(away, way, 2 + place, 0, 8))
            row = 6 + place % 2
            parts.append(rows_of(away, way, place // 2, row, row + 1))
        indices = halves(names[0], turn(names[1])).astype(jnp.int32)
        shares = halves(turn(names[0]), names[1])
        parts = (halves(parts[0], turn(parts[1])), halves(turn(parts[0]), parts[1]))
        sums = [jnp.zeros((8, LANES), jnp.float32) for _ in range(2)]
        for side in range(6):
            index, share = wide(indices[side : side + 1]), wide(shares[side : side + 1])
            low, high = index & 127, index >> 7
            here = jnp.where(high == spot, share, 0.0)
            for level in range(2):
                got = halves(pick(tables[level], low), pick(tables[2 + level], low))
                sums[level] = sums[level] + here * got
        for level in range(2):
            cell_ref[2 + level, group : group + 1, :] = total(sums[level]) + parts[level]

    halo = split(halo_ref[...].reshape(6 * 8, LANES), 0)
    counts = counting()

    def edges(step, carry):
        columns = pl.ds(pl.multiple_of(step * SPAN, SPAN), SPAN)
        sums = [[sums_ref[step * 2 + half, field] for field in range(6)] for half in range(2)]
        for side in range(10):
            index, weight = near_ref[side : side + 1, columns], weight_ref[side : side + 1, columns]
            got = product(halo, ones_at(index, counts))
            got = got[:48] + got[48:]
            for half in range(2):
                part_of = slice(half * LANES, (half + 1) * LANES)
                high = wide(index[:, part_of]) >> 7
                here = jnp.where(high == spot + ROWS, wide(weight[:, part_of]), 0.0)
                for field in range(6):
                    values = got[field * 8 : field * 8 + 8, part_of]
                    sums[half][field] = sums[half][field] + here * values
        for half in range(2):
            block = step * 2 + half
            columns = pl.ds(pl.multiple_of(block * LANES, LANES), LANES)
            slopes = [jnp.zeros((8, LANES), jnp.float32) for _ in range(2)]
            for side in range(2):
                sign = 1.0 if side == 1 else -1.0
                index = wide(ends_ref[side : side + 1, columns])
                low, high = index & 127, index >> 7
                for part in range(2):
                    here = high == spot + BLOCKS * part
                    for level in range(2):
                        got = jnp.where(here, pick(cell_ref[2 * part + level], low), 0.0)
                        slopes[level] = slopes[level] + sign * got
            inverse = wide(inverse_ref[:, columns])
            row, tile = block % 8, block // 8
            below = around_ref[0, EDGE + core * 3 + tile, pl.ds(row, 1), :]
            above = around_ref[1, EDGE + core * 3 + tile, pl.ds(row, 1), :]
            speeds = [speed_ref[level : level + 1, columns] for level in range(2)]
            risers = [speeds[1] - below, above - speeds[0]]
            for level in range(2):
                vort = wide(vort_ref[level : level + 1, columns])
                flux = 0.5 * (vort * sums[half][2 + level] + sums[half][4 + level])
                result = total(flux - slopes[level] * inverse)
                advect = -0.5 * wind_ref[level : level + 1, columns] * risers[level]
                tendency_ref[level : level + 1, columns] = result + advect
                tangent_ref[level : level + 1, columns] = total(sums[half][level])
        return carry

    lax.fori_loop(0, ROWS // 2, edges, 0, unroll=True)


VMEM = pl.BlockSpec(memory_space=pltpu.VMEM)


def body(
    velocity,
    thickness,
    vorticity,
    vertical_wind,
    weights_on_edge,
    edges_on_edge,
    edges_on_cell,
    cells_on_edge,
    energy_weight,
    inverse_distance,
    edge_halo_list,
    edge_halo_count,
    cell_halo_list,
    cell_halo_count,
):
    del edge_halo_count, cell_halo_count
    f32 = jnp.float32
    core = lax.axis_index("core")
    params = pltpu.CompilerParams(vmem_limit_bytes=24 << 20)
    inputs = (
        velocity, thickness, vorticity, edge_halo_list, cell_halo_list, edges_on_cell, energy_weight
    )
    sent, tables = pl.pallas_call(
        pack_kernel,
        out_shape=(
            jax.ShapeDtypeStruct((TILES, 8, LANES), f32),
            jax.ShapeDtypeStruct((18, 8, LANES), f32),
        ),
        in_specs=[pl.BlockSpec(memory_space=pltpu.HBM)] * 7,
        out_specs=(VMEM, VMEM),
        scratch_shapes=[pltpu.VMEM(x.shape, x.dtype) for x in inputs]
        + [pltpu.VMEM((8, LANES), jnp.int32), pltpu.SemaphoreType.DMA((7,))],
        compiler_params=params,
        name="pack",
    )(*(pltpu.with_memory_space_constraint(x, pltpu.HBM) for x in inputs))

    mesh_axes = ("x", "z", "core")
    own = lax.all_gather(sent, "core")
    even = core == 0
    z = lax.axis_index("z")
    corner = lax.axis_index("x") + lax.axis_index("lev") + z == 0
    early = ((z < EARLY) & ~corner).astype(jnp.int32).reshape(1)
    own, tables = lax.optimization_barrier((own, tables))
    operands = (tables, edges_on_edge, weights_on_edge)
    flag = pl.BlockSpec(memory_space=pltpu.SMEM)
    sums_shape = jax.ShapeDtypeStruct((ROWS, 6, 8, LANES), f32)
    made = pl.pallas_call(
        local_early_kernel,
        out_shape=sums_shape,
        in_specs=[flag] + [VMEM] * 3,
        out_specs=VMEM,
        compiler_params=params,
        name="local_early",
    )(early, *operands)
    own, made = lax.optimization_barrier((own, made))
    near = jnp.where(even, own[:, :WAY], own[:, WAY:RIM])
    rims = jnp.where(even, own[:, RIM + 3 :], own[:, RIM : RIM + 3])
    chips = lax.axis_size("x") * lax.axis_size("z")

    def apart(block, distance):
        right = [(2 * c, 2 * ((c + distance) % chips)) for c in range(chips)]
        left = [(2 * c + 1, 2 * ((c - distance) % chips) + 1) for c in range(chips)]
        return lax.ppermute(block, mesh_axes, right + left)

    groups = lax.axis_size("lev")
    up = [(i, i + 1) for i in range(groups - 1)]
    down = [(groups + i + 1, groups + i) for i in range(groups - 1)]
    speeds = near[:, :2].reshape(4, 8, LANES)
    rest = jnp.where(even, near[1, 4:], near[0, 4:])
    spare = near[1]
    arrived = [
        apart(near, 1).reshape(12, 8, LANES),
        apart(jnp.concatenate([speeds, rest, spare[:2]], axis=0), 2),
        apart(jnp.concatenate([speeds, spare[:3]], axis=0), 3),
        lax.ppermute(rims, ("core", "lev"), up + down).reshape(6, 8, LANES),
    ]
    arrived = jnp.concatenate(arrived, axis=0)
    sums, energy_sums = pl.pallas_call(
        local_late_kernel,
        out_shape=(sums_shape, jax.ShapeDtypeStruct((BLOCKS, 2, 8, LANES), f32)),
        in_specs=[flag] + [VMEM] * 6,
        out_specs=(VMEM, VMEM),
        compiler_params=params,
        cost_estimate=pl.CostEstimate(flops=20_000_000, bytes_accessed=1_000_000, transcendentals=0),
        name="local_late",
    )(early, made, *operands, edges_on_cell, energy_weight)
    around = lax.all_gather(arrived, "core")
    return pl.pallas_call(
        finish_kernel,
        out_shape=(
            jax.ShapeDtypeStruct(velocity.shape, f32),
            jax.ShapeDtypeStruct(velocity.shape, f32),
            jax.ShapeDtypeStruct((velocity.shape[0], edges_on_cell.shape[1]), f32),
        ),
        in_specs=[pl.BlockSpec(memory_space=pltpu.SMEM)] + [VMEM] * 13,
        out_specs=(VMEM, VMEM, VMEM),
        scratch_shapes=[pltpu.VMEM((6, 8, LANES), f32), pltpu.VMEM((4, 8, LANES), f32)],
        compiler_params=params,
        name="finish",
    )(
        core.astype(jnp.int32).reshape(1), own, around, sums, energy_sums, edges_on_edge, weights_on_edge,
        edges_on_cell, energy_weight, cells_on_edge, inverse_distance.reshape(1, -1), vorticity,
        vertical_wind, velocity,
    )


def solution(mesh):
    fine = Mesh(mesh.devices.reshape(4, 12, 2, 8), ("x", "z", "core", "lev"))
    parts = ("x", "z", "core")
    in_specs = (
        P("lev", parts),
        P("lev", parts),
        P("lev", parts),
        P("lev", parts),
        P(None, parts),
        P(None, parts),
        P(None, parts),
        P(None, parts),
        P(None, parts),
        P(parts),
        P(parts, None),
        P(parts),
        P(parts, None),
        P(parts),
    )
    out_specs = (P("lev", parts), P("lev", parts), P("lev", parts))
    return jax.shard_map(body, mesh=fine, in_specs=in_specs, out_specs=out_specs, check_vma=False)
```

```python
import jax
import jax.numpy as jnp
from jax import lax
from jax.experimental import pallas as pl
from jax.experimental.pallas import tpu as pltpu
from jax.sharding import Mesh, PartitionSpec as P

OFF = (1, 2, 3, -1, -2, -3)
LANES = 128
ROWS = 24
LOCAL = ROWS * LANES
BLOCKS = 8

WAY = 6
RIM = 2 * WAY
TILES = RIM + 6
EARLY = 4
NEAR, MIDDLE, FAR, EDGE = 0, 12, 20, 27


def pick(table, low):
    return jnp.take_along_axis(table, low, axis=1, mode="promise_in_bounds")


def wide(row):
    return jnp.broadcast_to(row, (8, LANES))


def sublanes():
    return lax.broadcasted_iota(jnp.int32, (8, LANES), 0)


def total(tile):
    return jnp.sum(tile, axis=0, keepdims=True)


SPAN = 2 * LANES


def split(table, axis):
    coarse = table.astype(jnp.bfloat16)
    fine = (table - coarse.astype(jnp.float32)).astype(jnp.bfloat16)
    return jnp.concatenate([coarse, fine], axis=axis)


def ones_at(index, counts):
    low = (index & 127).astype(jnp.float32).astype(jnp.bfloat16)
    here = counts == jnp.broadcast_to(low, (LANES, SPAN))
    return jnp.where(here, jnp.bfloat16(1), jnp.bfloat16(0))


def product(table, ones):
    return jnp.dot(table, ones, preferred_element_type=jnp.float32)


def counting():
    return lax.broadcasted_iota(jnp.int32, (LANES, SPAN), 0).astype(jnp.float32).astype(jnp.bfloat16)


def halves(left, right):
    lane = lax.broadcasted_iota(jnp.int32, left.shape, 1)
    return jnp.where(lane < 64, left, right)


def turn(tile):
    return pltpu.roll(tile, 64, 1)


def pack_kernel(
    speed_hbm, height_hbm, vort_hbm, edge_list_hbm, cell_list_hbm, cells_hbm, share_hbm,
    sent_ref, table_ref,
    speed_ref, height_ref, vort_ref, edge_list_ref, cell_list_ref, cells_ref, share_ref, pair_ref, done,
):
    pairs = (
        (speed_hbm, speed_ref), (height_hbm, height_ref), (vort_hbm, vort_ref), (edge_list_hbm, edge_list_ref),
        (cell_list_hbm, cell_list_ref), (cells_hbm, cells_ref), (share_hbm, share_ref),
    )
    copies = [pltpu.make_async_copy(src, dst, done.at[i]) for i, (src, dst) in enumerate(pairs)]
    for copy in copies:
        copy.start()
    for way in range(2):
        for tile in (0, 1, 5):
            sent_ref[way * WAY + tile] = jnp.zeros((8, LANES), jnp.float32)
    for copy in copies[:3]:
        copy.wait()
    for level in range(2):
        for row in range(ROWS):
            tile, place = level * 3 + row // 8, slice(row % 8, row % 8 + 1)
            columns = slice(row * LANES, (row + 1) * LANES)
            table_ref[tile, place, :] = speed_ref[level : level + 1, columns]
            table_ref[6 + tile, place, :] = height_ref[level : level + 1, columns]
            table_ref[12 + tile, place, :] = vort_ref[level : level + 1, columns]
    for tile in range(6):
        speed = table_ref[tile]
        mass = speed * table_ref[6 + tile]
        table_ref[6 + tile] = mass
        table_ref[12 + tile] = mass * table_ref[12 + tile]
        sent_ref[RIM + tile] = speed
    spot = sublanes()
    copies[3].wait()
    for block in range(6):
        index = wide(edge_list_ref[block : block + 1, :])
        low, high = index & 127, index >> 7
        way, place = WAY * (block // 3), block % 3
        for field in range(6):
            found = jnp.zeros((8, LANES), jnp.float32)
            for part in range(3):
                got = pick(table_ref[field * 3 + part], low)
                found = jnp.where(high == spot + 8 * part, got, found)
            row, level = total(found), field % 2
            if field < 2:
                sent_ref[level, block : block + 1, :] = row
                sent_ref[WAY + level, block : block + 1, :] = row
            elif field < 4:
                sent_ref[way + 2 + place, 6 + level : 7 + level, :] = row
            else:
                sent_ref[way + 5, level * 3 + place : level * 3 + place + 1, :] = row
    for copy in copies[4:]:
        copy.wait()
    pair_ref[...] = jnp.zeros((8, LANES), jnp.int32)
    for block in range(6):
        pair_ref[block : block + 1, 0:64] = cell_list_ref[block : block + 1, :]
    lists = pair_ref[...]
    turned = turn(lists)
    for group in range(3):
        index = wide(lists[2 * group : 2 * group + 1] + turned[2 * group + 1 : 2 * group + 2])
        low, high = index[:6] & 127, index[:6] >> 7
        edges = jnp.zeros((6, LANES), jnp.int32)
        shares = jnp.zeros((6, LANES), jnp.float32)
        for block in range(BLOCKS):
            columns = slice(block * LANES, (block + 1) * LANES)
            here = high == block
            edges = jnp.where(here, pick(cells_ref[:, columns], low), edges)
            shares = jnp.where(here, pick(share_ref[:, columns], low), shares)
        names = (edges - LOCAL).astype(jnp.float32)
        tables = (halves(names, turn(shares)), halves(turn(names), shares))
        sums = [jnp.zeros((8, LANES), jnp.float32) for _ in range(2)]
        for side in range(6):
            index, share = wide(edges[side : side + 1]), wide(shares[side : side + 1])
            low, high = index & 127, index >> 7
            for part in range(3):
                weight = jnp.where(high == spot + 8 * part, share, 0.0)
                for level in range(2):
                    got = pick(table_ref[level * 3 + part], low)
                    sums[level] = sums[level] + weight * (got * got)
        sums = [total(part) for part in sums]
        parts = (halves(sums[0], turn(sums[1])), halves(turn(sums[0]), sums[1]))
        for half in range(2):
            block = 2 * group + half
            way, place = WAY * (block // 3), block % 3
            sent_ref[way + 2 + place, 0:6, :] = tables[half]
            row = 6 + place % 2
            sent_ref[way + place // 2, row : row + 1, :] = parts[half]


def local_early_kernel(early_ref, table_ref, near_ref, weight_ref, sums_ref):
    @pl.when(early_ref[0] == 1)
    def _():
        local_sums(table_ref, near_ref, weight_ref, sums_ref)


def local_late_kernel(
    early_ref, made_ref, table_ref, near_ref, weight_ref, cells_ref, share_ref, sums_ref, energy_ref,
):
    @pl.when(early_ref[0] == 1)
    def _():
        sums_ref[...] = made_ref[...]
        cell_sums(table_ref, cells_ref, share_ref, energy_ref)

    @pl.when(early_ref[0] == 0)
    def _():
        local_sums(table_ref, near_ref, weight_ref, sums_ref)
        cell_sums(table_ref, cells_ref, share_ref, energy_ref)


def local_sums(table_ref, near_ref, weight_ref, sums_ref):
    spot = sublanes()
    table = split(table_ref[...].reshape(18 * 8, LANES), 1)
    counts = counting()

    def edges(step, carry):
        columns = pl.ds(pl.multiple_of(step * SPAN, SPAN), SPAN)
        sums = [[jnp.zeros((8, LANES), jnp.float32) for _ in range(6)] for _ in range(2)]
        for side in range(10):
            index, weight = near_ref[side : side + 1, columns], weight_ref[side : side + 1, columns]
            ones = ones_at(index, counts)
            got = product(table, jnp.concatenate([ones, ones], axis=0))
            for half in range(2):
                part_of = slice(half * LANES, (half + 1) * LANES)
                high = wide(index[:, part_of]) >> 7
                share = wide(weight[:, part_of])
                for part in range(3):
                    here = jnp.where(high == spot + 8 * part, share, 0.0)
                    for field in range(6):
                        row = (field * 3 + part) * 8
                        sums[half][field] = sums[half][field] + here * got[row : row + 8, part_of]
        for half in range(2):
            for field in range(6):
                sums_ref[step * 2 + half, field] = sums[half][field]
        return carry

    lax.fori_loop(0, ROWS // 2, edges, 0, unroll=True)


def cell_sums(table_ref, cells_ref, share_ref, energy_ref):
    spot = sublanes()

    def cells(step, carry):
        columns = pl.ds(pl.multiple_of(step * LANES, LANES), LANES)
        sums = [jnp.zeros((8, LANES), jnp.float32) for _ in range(2)]
        for side in range(6):
            index = wide(cells_ref[side : side + 1, columns])
            share = wide(share_ref[side : side + 1, columns])
            low, high = index & 127, index >> 7
            for part in range(3):
                here = jnp.where(high == spot + 8 * part, share, 0.0)
                for level in range(2):
                    got = pick(table_ref[level * 3 + part], low)
                    sums[level] = sums[level] + here * (got * got)
        for level in range(2):
            energy_ref[step, level] = sums[level]
        return carry

    lax.fori_loop(0, BLOCKS, cells, 0, unroll=True)


def finish_kernel(
    core_ref, own_ref, around_ref, sums_ref, energy_sums_ref, near_ref, weight_ref, cells_ref, share_ref,
    ends_ref, inverse_ref, vort_ref, wind_ref, speed_ref, tendency_ref, tangent_ref, energy_ref,
    halo_ref, cell_ref,
):
    core = core_ref[0]
    first = jnp.full((8, LANES), core, jnp.int32) == 0
    spot = sublanes()

    def rows_at(way, tile, rows, place):
        chip, part = place // 2, place % 2
        side = 0 if chip < 0 else 1
        if chip == 0:
            return own_ref[part, way * WAY + tile, rows, :]
        if abs(chip) == 1:
            at = NEAR + part * WAY + tile
        elif abs(chip) == 2 and tile < 2:
            at = MIDDLE + part * 2 + tile
        elif abs(chip) == 2:
            assert part == 1 - side and tile >= 4
            at = MIDDLE + tile
        else:
            assert abs(chip) == 3 and tile < 2
            at = FAR + part * 2 + tile
        return around_ref[side, at, rows, :]

    def rows_of(distance, way, tile, start, stop):
        rows = slice(start, stop)
        on_first = rows_at(way, tile, rows, distance)
        on_second = rows_at(way, tile, rows, distance + 1)
        return jnp.where(first[: stop - start], on_first, on_second)

    for field in range(6):
        halo_ref[field] = jnp.zeros((8, LANES), jnp.float32)
    for block in range(6):
        away, way, place = -OFF[block], block // 3, block % 3
        mass = rows_of(away, way, 2 + place, 6, 8)
        for level in range(2):
            row = slice(block, block + 1)
            halo_ref[level, row, :] = rows_of(away, way, level, block, block + 1)
            halo_ref[2 + level, row, :] = mass[level : level + 1]
            at = level * 3 + place
            halo_ref[4 + level, row, :] = rows_of(away, way, 5, at, at + 1)

    squares = [halo_ref[level] * halo_ref[level] for level in range(2)]
    for step in range(BLOCKS):
        columns = slice(step * LANES, (step + 1) * LANES)
        sums = [energy_sums_ref[step, level] for level in range(2)]
        for side in range(6):
            index = wide(cells_ref[side : side + 1, columns])
            share = wide(share_ref[side : side + 1, columns])
            low, high = index & 127, index >> 7
            here = jnp.where(high == spot + ROWS, share, 0.0)
            for level in range(2):
                sums[level] = sums[level] + here * pick(squares[level], low)
        for level in range(2):
            row = total(sums[level])
            energy_ref[level : level + 1, columns] = row
            cell_ref[level, step : step + 1, :] = row

    for level in range(2):
        cell_ref[2 + level] = jnp.zeros((8, LANES), jnp.float32)
    for group in range(3):
        tables, names, parts = [], [], []
        for half in range(2):
            block = 2 * group + half
            away, way, place = -OFF[block], block // 3, block % 3
            for level in range(2):
                table = jnp.zeros((8, LANES), jnp.float32)
                for sender in range(6):
                    table = jnp.where(spot == sender, rows_of(away - OFF[sender], 0, level, 0, 8), table)
                tables.append(table * table)
            names.append(rows_of(away, way, 2 + place, 0, 8))
            row = 6 + place % 2
            parts.append(rows_of(away, way, place // 2, row, row + 1))
        indices = halves(names[0], turn(names[1])).astype(jnp.int32)
        shares = halves(turn(names[0]), names[1])
        parts = (halves(parts[0], turn(parts[1])), halves(turn(parts[0]), parts[1]))
        sums = [jnp.zeros((8, LANES), jnp.float32) for _ in range(2)]
        for side in range(6):
            index, share = wide(indices[side : side + 1]), wide(shares[side : side + 1])
            low, high = index & 127, index >> 7
            here = jnp.where(high == spot, share, 0.0)
            for level in range(2):
                got = halves(pick(tables[level], low), pick(tables[2 + level], low))
                sums[level] = sums[level] + here * got
        for level in range(2):
            cell_ref[2 + level, group : group + 1, :] = total(sums[level]) + parts[level]

    halo = split(halo_ref[...].reshape(6 * 8, LANES), 0)
    counts = counting()

    def edges(step, carry):
        columns = pl.ds(pl.multiple_of(step * SPAN, SPAN), SPAN)
        sums = [[sums_ref[step * 2 + half, field] for field in range(6)] for half in range(2)]
        for side in range(10):
            index, weight = near_ref[side : side + 1, columns], weight_ref[side : side + 1, columns]
            got = product(halo, ones_at(index, counts))
            got = got[:48] + got[48:]
            for half in range(2):
                part_of = slice(half * LANES, (half + 1) * LANES)
                high = wide(index[:, part_of]) >> 7
                here = jnp.where(high == spot + ROWS, wide(weight[:, part_of]), 0.0)
                for field in range(6):
                    values = got[field * 8 : field * 8 + 8, part_of]
                    sums[half][field] = sums[half][field] + here * values
        for half in range(2):
            block = step * 2 + half
            columns = pl.ds(pl.multiple_of(block * LANES, LANES), LANES)
            slopes = [jnp.zeros((8, LANES), jnp.float32) for _ in range(2)]
            for side in range(2):
                sign = 1.0 if side == 1 else -1.0
                index = wide(ends_ref[side : side + 1, columns])
                low, high = index & 127, index >> 7
                for part in range(2):
                    here = high == spot + BLOCKS * part
                    for level in range(2):
                        got = jnp.where(here, pick(cell_ref[2 * part + level], low), 0.0)
                        slopes[level] = slopes[level] + sign * got
            inverse = wide(inverse_ref[:, columns])
            row, tile = block % 8, block // 8
            below = around_ref[0, EDGE + core * 3 + tile, pl.ds(row, 1), :]
            above = around_ref[1, EDGE + core * 3 + tile, pl.ds(row, 1), :]
            speeds = [speed_ref[level : level + 1, columns] for level in range(2)]
            risers = [speeds[1] - below, above - speeds[0]]
            for level in range(2):
                vort = wide(vort_ref[level : level + 1, columns])
                flux = 0.5 * (vort * sums[half][2 + level] + sums[half][4 + level])
                result = total(flux - slopes[level] * inverse)
                advect = -0.5 * wind_ref[level : level + 1, columns] * risers[level]
                tendency_ref[level : level + 1, columns] = result + advect
                tangent_ref[level : level + 1, columns] = total(sums[half][level])
        return carry

    lax.fori_loop(0, ROWS // 2, edges, 0, unroll=True)


VMEM = pl.BlockSpec(memory_space=pltpu.VMEM)


def body(
    velocity,
    thickness,
    vorticity,
    vertical_wind,
    weights_on_edge,
    edges_on_edge,
    edges_on_cell,
    cells_on_edge,
    energy_weight,
    inverse_distance,
    edge_halo_list,
    edge_halo_count,
    cell_halo_list,
    cell_halo_count,
):
    del edge_halo_count, cell_halo_count
    f32 = jnp.float32
    core = lax.axis_index("core")
    params = pltpu.CompilerParams(vmem_limit_bytes=24 << 20)
    inputs = (
        velocity, thickness, vorticity, edge_halo_list, cell_halo_list, edges_on_cell, energy_weight
    )
    sent, tables = pl.pallas_call(
        pack_kernel,
        out_shape=(
            jax.ShapeDtypeStruct((TILES, 8, LANES), f32),
            jax.ShapeDtypeStruct((18, 8, LANES), f32),
        ),
        in_specs=[pl.BlockSpec(memory_space=pltpu.HBM)] * 7,
        out_specs=(VMEM, VMEM),
        scratch_shapes=[pltpu.VMEM(x.shape, x.dtype) for x in inputs]
        + [pltpu.VMEM((8, LANES), jnp.int32), pltpu.SemaphoreType.DMA((7,))],
        compiler_params=params,
        name="pack",
    )(*(pltpu.with_memory_space_constraint(x, pltpu.HBM) for x in inputs))

    mesh_axes = ("x", "z", "core")
    own = lax.all_gather(sent, "core")
    even = core == 0
    z = lax.axis_index("z")
    corner = lax.axis_index("x") + lax.axis_index("lev") + z == 0
    early = ((z < EARLY) & ~corner).astype(jnp.int32).reshape(1)
    own, tables = lax.optimization_barrier((own, tables))
    operands = (tables, edges_on_edge, weights_on_edge)
    flag = pl.BlockSpec(memory_space=pltpu.SMEM)
    sums_shape = jax.ShapeDtypeStruct((ROWS, 6, 8, LANES), f32)
    made = pl.pallas_call(
        local_early_kernel,
        out_shape=sums_shape,
        in_specs=[flag] + [VMEM] * 3,
        out_specs=VMEM,
        compiler_params=params,
        name="local_early",
    )(early, *operands)
    own, made = lax.optimization_barrier((own, made))
    near = jnp.where(even, own[:, :WAY], own[:, WAY:RIM])
    rims = jnp.where(even, own[:, RIM + 3 :], own[:, RIM : RIM + 3])
    chips = lax.axis_size("x") * lax.axis_size("z")

    def apart(block, distance):
        right = [(2 * c, 2 * ((c + distance) % chips)) for c in range(chips)]
        left = [(2 * c + 1, 2 * ((c - distance) % chips) + 1) for c in range(chips)]
        return lax.ppermute(block, mesh_axes, right + left)

    groups = lax.axis_size("lev")
    up = [(i, i + 1) for i in range(groups - 1)]
    down = [(groups + i + 1, groups + i) for i in range(groups - 1)]
    speeds = near[:, :2].reshape(4, 8, LANES)
    rest = jnp.where(even, near[1, 4:], near[0, 4:])
    spare = near[1]
    arrived = [
        apart(near, 1).reshape(12, 8, LANES),
        apart(jnp.concatenate([speeds, rest, spare[:2]], axis=0), 2),
        apart(jnp.concatenate([speeds, spare[:3]], axis=0), 3),
        lax.ppermute(rims, ("core", "lev"), up + down).reshape(6, 8, LANES),
    ]
    arrived = jnp.concatenate(arrived, axis=0)
    sums, energy_sums = pl.pallas_call(
        local_late_kernel,
        out_shape=(sums_shape, jax.ShapeDtypeStruct((BLOCKS, 2, 8, LANES), f32)),
        in_specs=[flag] + [VMEM] * 6,
        out_specs=(VMEM, VMEM),
        compiler_params=params,
        cost_estimate=pl.CostEstimate(flops=20_000_000, bytes_accessed=1_000_000, transcendentals=0),
        name="local_late",
    )(early, made, *operands, edges_on_cell, energy_weight)
    around = lax.all_gather(arrived, "core")
    return pl.pallas_call(
        finish_kernel,
        out_shape=(
            jax.ShapeDtypeStruct(velocity.shape, f32),
            jax.ShapeDtypeStruct(velocity.shape, f32),
            jax.ShapeDtypeStruct((velocity.shape[0], edges_on_cell.shape[1]), f32),
        ),
        in_specs=[pl.BlockSpec(memory_space=pltpu.SMEM)] + [VMEM] * 13,
        out_specs=(VMEM, VMEM, VMEM),
        scratch_shapes=[pltpu.VMEM((6, 8, LANES), f32), pltpu.VMEM((4, 8, LANES), f32)],
        compiler_params=params,
        name="finish",
    )(
        core.astype(jnp.int32).reshape(1), own, around, sums, energy_sums, edges_on_edge, weights_on_edge,
        edges_on_cell, energy_weight, cells_on_edge, inverse_distance.reshape(1, -1), vorticity,
        vertical_wind, velocity,
    )


def solution(mesh):
    fine = Mesh(mesh.devices.reshape(4, 12, 2, 8), ("x", "z", "core", "lev"))
    parts = ("x", "z", "core")
    in_specs = (
        P("lev", parts),
        P("lev", parts),
        P("lev", parts),
        P("lev", parts),
        P(None, parts),
        P(None, parts),
        P(None, parts),
        P(None, parts),
        P(None, parts),
        P(parts),
        P(parts, None),
        P(parts),
        P(parts, None),
        P(parts),
    )
    out_specs = (P("lev", parts), P("lev", parts), P("lev", parts))
    return jax.shard_map(body, mesh=fine, in_specs=in_specs, out_specs=out_specs, check_vma=False)
```

```python
import jax
import jax.numpy as jnp
from jax import lax
from jax.experimental import pallas as pl
from jax.experimental.pallas import tpu as pltpu
from jax.sharding import Mesh, PartitionSpec as P

OFF = (1, 2, 3, -1, -2, -3)
LANES = 128
ROWS = 24
LOCAL = ROWS * LANES
BLOCKS = 8

WAY = 6
RIM = 2 * WAY
TILES = RIM + 6
EARLY = 3
NEAR, MIDDLE, FAR, EDGE = 0, 12, 20, 27


def pick(table, low):
    return jnp.take_along_axis(table, low, axis=1, mode="promise_in_bounds")


def wide(row):
    return jnp.broadcast_to(row, (8, LANES))


def sublanes():
    return lax.broadcasted_iota(jnp.int32, (8, LANES), 0)


def total(tile):
    return jnp.sum(tile, axis=0, keepdims=True)


SPAN = 2 * LANES


def split(table, axis):
    coarse = table.astype(jnp.bfloat16)
    fine = (table - coarse.astype(jnp.float32)).astype(jnp.bfloat16)
    return jnp.concatenate([coarse, fine], axis=axis)


def ones_at(index, counts):
    low = (index & 127).astype(jnp.float32).astype(jnp.bfloat16)
    here = counts == jnp.broadcast_to(low, (LANES, SPAN))
    return jnp.where(here, jnp.bfloat16(1), jnp.bfloat16(0))


def product(table, ones):
    return jnp.dot(table, ones, preferred_element_type=jnp.float32)


def counting():
    return lax.broadcasted_iota(jnp.int32, (LANES, SPAN), 0).astype(jnp.float32).astype(jnp.bfloat16)


def halves(left, right):
    lane = lax.broadcasted_iota(jnp.int32, left.shape, 1)
    return jnp.where(lane < 64, left, right)


def turn(tile):
    return pltpu.roll(tile, 64, 1)


def pack_kernel(
    speed_hbm, height_hbm, vort_hbm, edge_list_hbm, cell_list_hbm, cells_hbm, share_hbm,
    sent_ref, table_ref,
    speed_ref, height_ref, vort_ref, edge_list_ref, cell_list_ref, cells_ref, share_ref, pair_ref, done,
):
    pairs = (
        (speed_hbm, speed_ref), (height_hbm, height_ref), (vort_hbm, vort_ref), (edge_list_hbm, edge_list_ref),
        (cell_list_hbm, cell_list_ref), (cells_hbm, cells_ref), (share_hbm, share_ref),
    )
    copies = [pltpu.make_async_copy(src, dst, done.at[i]) for i, (src, dst) in enumerate(pairs)]
    for copy in copies:
        copy.start()
    for way in range(2):
        for tile in (0, 1, 5):
            sent_ref[way * WAY + tile] = jnp.zeros((8, LANES), jnp.float32)
    for copy in copies[:3]:
        copy.wait()
    for level in range(2):
        for row in range(ROWS):
            tile, place = level * 3 + row // 8, slice(row % 8, row % 8 + 1)
            columns = slice(row * LANES, (row + 1) * LANES)
            table_ref[tile, place, :] = speed_ref[level : level + 1, columns]
            table_ref[6 + tile, place, :] = height_ref[level : level + 1, columns]
            table_ref[12 + tile, place, :] = vort_ref[level : level + 1, columns]
    for tile in range(6):
        speed = table_ref[tile]
        mass = speed * table_ref[6 + tile]
        table_ref[6 + tile] = mass
        table_ref[12 + tile] = mass * table_ref[12 + tile]
        sent_ref[RIM + tile] = speed
    spot = sublanes()
    copies[3].wait()
    for block in range(6):
        index = wide(edge_list_ref[block : block + 1, :])
        low, high = index & 127, index >> 7
        way, place = WAY * (block // 3), block % 3
        for field in range(6):
            found = jnp.zeros((8, LANES), jnp.float32)
            for part in range(3):
                got = pick(table_ref[field * 3 + part], low)
                found = jnp.where(high == spot + 8 * part, got, found)
            row, level = total(found), field % 2
            if field < 2:
                sent_ref[level, block : block + 1, :] = row
                sent_ref[WAY + level, block : block + 1, :] = row
            elif field < 4:
                sent_ref[way + 2 + place, 6 + level : 7 + level, :] = row
            else:
                sent_ref[way + 5, level * 3 + place : level * 3 + place + 1, :] = row
    for copy in copies[4:]:
        copy.wait()
    pair_ref[...] = jnp.zeros((8, LANES), jnp.int32)
    for block in range(6):
        pair_ref[block : block + 1, 0:64] = cell_list_ref[block : block + 1, :]
    lists = pair_ref[...]
    turned = turn(lists)
    for group in range(3):
        index = wide(lists[2 * group : 2 * group + 1] + turned[2 * group + 1 : 2 * group + 2])
        low, high = index[:6] & 127, index[:6] >> 7
        edges = jnp.zeros((6, LANES), jnp.int32)
        shares = jnp.zeros((6, LANES), jnp.float32)
        for block in range(BLOCKS):
            columns = slice(block * LANES, (block + 1) * LANES)
            here = high == block
            edges = jnp.where(here, pick(cells_ref[:, columns], low), edges)
            shares = jnp.where(here, pick(share_ref[:, columns], low), shares)
        names = (edges - LOCAL).astype(jnp.float32)
        tables = (halves(names, turn(shares)), halves(turn(names), shares))
        sums = [jnp.zeros((8, LANES), jnp.float32) for _ in range(2)]
        for side in range(6):
            index, share = wide(edges[side : side + 1]), wide(shares[side : side + 1])
            low, high = index & 127, index >> 7
            for part in range(3):
                weight = jnp.where(high == spot + 8 * part, share, 0.0)
                for level in range(2):
                    got = pick(table_ref[level * 3 + part], low)
                    sums[level] = sums[level] + weight * (got * got)
        sums = [total(part) for part in sums]
        parts = (halves(sums[0], turn(sums[1])), halves(turn(sums[0]), sums[1]))
        for half in range(2):
            block = 2 * group + half
            way, place = WAY * (block // 3), block % 3
            sent_ref[way + 2 + place, 0:6, :] = tables[half]
            row = 6 + place % 2
            sent_ref[way + place // 2, row : row + 1, :] = parts[half]


def local_early_kernel(early_ref, table_ref, near_ref, weight_ref, sums_ref):
    @pl.when(early_ref[0] == 1)
    def _():
        local_sums(table_ref, near_ref, weight_ref, sums_ref)


def local_late_kernel(
    early_ref, made_ref, table_ref, near_ref, weight_ref, cells_ref, share_ref, sums_ref, energy_ref,
):
    @pl.when(early_ref[0] == 1)
    def _():
        sums_ref[...] = made_ref[...]
        cell_sums(table_ref, cells_ref, share_ref, energy_ref)

    @pl.when(early_ref[0] == 0)
    def _():
        local_sums(table_ref, near_ref, weight_ref, sums_ref)
        cell_sums(table_ref, cells_ref, share_ref, energy_ref)


def local_sums(table_ref, near_ref, weight_ref, sums_ref):
    spot = sublanes()
    table = split(table_ref[...].reshape(18 * 8, LANES), 1)
    counts = counting()

    def edges(step, carry):
        columns = pl.ds(pl.multiple_of(step * SPAN, SPAN), SPAN)
        sums = [[jnp.zeros((8, LANES), jnp.float32) for _ in range(6)] for _ in range(2)]
        for side in range(10):
            index, weight = near_ref[side : side + 1, columns], weight_ref[side : side + 1, columns]
            ones = ones_at(index, counts)
            got = product(table, jnp.concatenate([ones, ones], axis=0))
            for half in range(2):
                part_of = slice(half * LANES, (half + 1) * LANES)
                high = wide(index[:, part_of]) >> 7
                share = wide(weight[:, part_of])
                for part in range(3):
                    here = jnp.where(high == spot + 8 * part, share, 0.0)
                    for field in range(6):
                        row = (field * 3 + part) * 8
                        sums[half][field] = sums[half][field] + here * got[row : row + 8, part_of]
        for half in range(2):
            for field in range(6):
                sums_ref[step * 2 + half, field] = sums[half][field]
        return carry

    lax.fori_loop(0, ROWS // 2, edges, 0, unroll=True)


def cell_sums(table_ref, cells_ref, share_ref, energy_ref):
    spot = sublanes()

    def cells(step, carry):
        columns = pl.ds(pl.multiple_of(step * LANES, LANES), LANES)
        sums = [jnp.zeros((8, LANES), jnp.float32) for _ in range(2)]
        for side in range(6):
            index = wide(cells_ref[side : side + 1, columns])
            share = wide(share_ref[side : side + 1, columns])
            low, high = index & 127, index >> 7
            for part in range(3):
                here = jnp.where(high == spot + 8 * part, share, 0.0)
                for level in range(2):
                    got = pick(table_ref[level * 3 + part], low)
                    sums[level] = sums[level] + here * (got * got)
        for level in range(2):
            energy_ref[step, level] = sums[level]
        return carry

    lax.fori_loop(0, BLOCKS, cells, 0, unroll=True)


def finish_kernel(
    core_ref, own_ref, around_ref, sums_ref, energy_sums_ref, near_ref, weight_ref, cells_ref, share_ref,
    ends_ref, inverse_ref, vort_ref, wind_ref, speed_ref, tendency_ref, tangent_ref, energy_ref,
    halo_ref, cell_ref,
):
    core = core_ref[0]
    first = jnp.full((8, LANES), core, jnp.int32) == 0
    spot = sublanes()

    def rows_at(way, tile, rows, place):
        chip, part = place // 2, place % 2
        side = 0 if chip < 0 else 1
        if chip == 0:
            return own_ref[part, way * WAY + tile, rows, :]
        if abs(chip) == 1:
            at = NEAR + part * WAY + tile
        elif abs(chip) == 2 and tile < 2:
            at = MIDDLE + part * 2 + tile
        elif abs(chip) == 2:
            assert part == 1 - side and tile >= 4
            at = MIDDLE + tile
        else:
            assert abs(chip) == 3 and tile < 2
            at = FAR + part * 2 + tile
        return around_ref[side, at, rows, :]

    def rows_of(distance, way, tile, start, stop):
        rows = slice(start, stop)
        on_first = rows_at(way, tile, rows, distance)
        on_second = rows_at(way, tile, rows, distance + 1)
        return jnp.where(first[: stop - start], on_first, on_second)

    for field in range(6):
        halo_ref[field] = jnp.zeros((8, LANES), jnp.float32)
    for block in range(6):
        away, way, place = -OFF[block], block // 3, block % 3
        mass = rows_of(away, way, 2 + place, 6, 8)
        for level in range(2):
            row = slice(block, block + 1)
            halo_ref[level, row, :] = rows_of(away, way, level, block, block + 1)
            halo_ref[2 + level, row, :] = mass[level : level + 1]
            at = level * 3 + place
            halo_ref[4 + level, row, :] = rows_of(away, way, 5, at, at + 1)

    squares = [halo_ref[level] * halo_ref[level] for level in range(2)]
    for step in range(BLOCKS):
        columns = slice(step * LANES, (step + 1) * LANES)
        sums = [energy_sums_ref[step, level] for level in range(2)]
        for side in range(6):
            index = wide(cells_ref[side : side + 1, columns])
            share = wide(share_ref[side : side + 1, columns])
            low, high = index & 127, index >> 7
            here = jnp.where(high == spot + ROWS, share, 0.0)
            for level in range(2):
                sums[level] = sums[level] + here * pick(squares[level], low)
        for level in range(2):
            row = total(sums[level])
            energy_ref[level : level + 1, columns] = row
            cell_ref[level, step : step + 1, :] = row

    for level in range(2):
        cell_ref[2 + level] = jnp.zeros((8, LANES), jnp.float32)
    for group in range(3):
        tables, names, parts = [], [], []
        for half in range(2):
            block = 2 * group + half
            away, way, place = -OFF[block], block // 3, block % 3
            for level in range(2):
                table = jnp.zeros((8, LANES), jnp.float32)
                for sender in range(6):
                    table = jnp.where(spot == sender, rows_of(away - OFF[sender], 0, level, 0, 8), table)
                tables.append(table * table)
            names.append(rows_of(away, way, 2 + place, 0, 8))
            row = 6 + place % 2
            parts.append(rows_of(away, way, place // 2, row, row + 1))
        indices = halves(names[0], turn(names[1])).astype(jnp.int32)
        shares = halves(turn(names[0]), names[1])
        parts = (halves(parts[0], turn(parts[1])), halves(turn(parts[0]), parts[1]))
        sums = [jnp.zeros((8, LANES), jnp.float32) for _ in range(2)]
        for side in range(6):
            index, share = wide(indices[side : side + 1]), wide(shares[side : side + 1])
            low, high = index & 127, index >> 7
            here = jnp.where(high == spot, share, 0.0)
            for level in range(2):
                got = halves(pick(tables[level], low), pick(tables[2 + level], low))
                sums[level] = sums[level] + here * got
        for level in range(2):
            cell_ref[2 + level, group : group + 1, :] = total(sums[level]) + parts[level]

    halo = split(halo_ref[...].reshape(6 * 8, LANES), 0)
    counts = counting()

    def edges(step, carry):
        columns = pl.ds(pl.multiple_of(step * SPAN, SPAN), SPAN)
        sums = [[sums_ref[step * 2 + half, field] for field in range(6)] for half in range(2)]
        for side in range(10):
            index, weight = near_ref[side : side + 1, columns], weight_ref[side : side + 1, columns]
            got = product(halo, ones_at(index, counts))
            got = got[:48] + got[48:]
            for half in range(2):
                part_of = slice(half * LANES, (half + 1) * LANES)
                high = wide(index[:, part_of]) >> 7
                here = jnp.where(high == spot + ROWS, wide(weight[:, part_of]), 0.0)
                for field in range(6):
                    values = got[field * 8 : field * 8 + 8, part_of]
                    sums[half][field] = sums[half][field] + here * values
        for half in range(2):
            block = step * 2 + half
            columns = pl.ds(pl.multiple_of(block * LANES, LANES), LANES)
            slopes = [jnp.zeros((8, LANES), jnp.float32) for _ in range(2)]
            for side in range(2):
                sign = 1.0 if side == 1 else -1.0
                index = wide(ends_ref[side : side + 1, columns])
                low, high = index & 127, index >> 7
                for part in range(2):
                    here = high == spot + BLOCKS * part
                    for level in range(2):
                        got = jnp.where(here, pick(cell_ref[2 * part + level], low), 0.0)
                        slopes[level] = slopes[level] + sign * got
            inverse = wide(inverse_ref[:, columns])
            row, tile = block % 8, block // 8
            below = around_ref[0, EDGE + core * 3 + tile, pl.ds(row, 1), :]
            above = around_ref[1, EDGE + core * 3 + tile, pl.ds(row, 1), :]
            speeds = [speed_ref[level : level + 1, columns] for level in range(2)]
            risers = [speeds[1] - below, above - speeds[0]]
            for level in range(2):
                vort = wide(vort_ref[level : level + 1, columns])
                flux = 0.5 * (vort * sums[half][2 + level] + sums[half][4 + level])
                result = total(flux - slopes[level] * inverse)
                advect = -0.5 * wind_ref[level : level + 1, columns] * risers[level]
                tendency_ref[level : level + 1, columns] = result + advect
                tangent_ref[level : level + 1, columns] = total(sums[half][level])
        return carry

    lax.fori_loop(0, ROWS // 2, edges, 0, unroll=True)


VMEM = pl.BlockSpec(memory_space=pltpu.VMEM)


def body(
    velocity,
    thickness,
    vorticity,
    vertical_wind,
    weights_on_edge,
    edges_on_edge,
    edges_on_cell,
    cells_on_edge,
    energy_weight,
    inverse_distance,
    edge_halo_list,
    edge_halo_count,
    cell_halo_list,
    cell_halo_count,
):
    del edge_halo_count, cell_halo_count
    f32 = jnp.float32
    core = lax.axis_index("core")
    params = pltpu.CompilerParams(vmem_limit_bytes=24 << 20)
    inputs = (
        velocity, thickness, vorticity, edge_halo_list, cell_halo_list, edges_on_cell, energy_weight
    )
    sent, tables = pl.pallas_call(
        pack_kernel,
        out_shape=(
            jax.ShapeDtypeStruct((TILES, 8, LANES), f32),
            jax.ShapeDtypeStruct((18, 8, LANES), f32),
        ),
        in_specs=[pl.BlockSpec(memory_space=pltpu.HBM)] * 7,
        out_specs=(VMEM, VMEM),
        scratch_shapes=[pltpu.VMEM(x.shape, x.dtype) for x in inputs]
        + [pltpu.VMEM((8, LANES), jnp.int32), pltpu.SemaphoreType.DMA((7,))],
        compiler_params=params,
        name="pack",
    )(*(pltpu.with_memory_space_constraint(x, pltpu.HBM) for x in inputs))

    mesh_axes = ("x", "z", "core")
    own = lax.all_gather(sent, "core")
    even = core == 0
    z = lax.axis_index("z")
    corner = lax.axis_index("x") + lax.axis_index("lev") + z == 0
    early = ((z < EARLY) & ~corner).astype(jnp.int32).reshape(1)
    own, tables = lax.optimization_barrier((own, tables))
    operands = (tables, edges_on_edge, weights_on_edge)
    flag = pl.BlockSpec(memory_space=pltpu.SMEM)
    sums_shape = jax.ShapeDtypeStruct((ROWS, 6, 8, LANES), f32)
    made = pl.pallas_call(
        local_early_kernel,
        out_shape=sums_shape,
        in_specs=[flag] + [VMEM] * 3,
        out_specs=VMEM,
        compiler_params=params,
        name="local_early",
    )(early, *operands)
    own, made = lax.optimization_barrier((own, made))
    near = jnp.where(even, own[:, :WAY], own[:, WAY:RIM])
    rims = jnp.where(even, own[:, RIM + 3 :], own[:, RIM : RIM + 3])
    chips = lax.axis_size("x") * lax.axis_size("z")

    def apart(block, distance):
        right = [(2 * c, 2 * ((c + distance) % chips)) for c in range(chips)]
        left = [(2 * c + 1, 2 * ((c - distance) % chips) + 1) for c in range(chips)]
        return lax.ppermute(block, mesh_axes, right + left)

    groups = lax.axis_size("lev")
    up = [(i, i + 1) for i in range(groups - 1)]
    down = [(groups + i + 1, groups + i) for i in range(groups - 1)]
    speeds = near[:, :2].reshape(4, 8, LANES)
    rest = jnp.where(even, near[1, 4:], near[0, 4:])
    spare = near[1]
    arrived = [
        apart(near, 1).reshape(12, 8, LANES),
        apart(jnp.concatenate([speeds, rest, spare[:2]], axis=0), 2),
        apart(jnp.concatenate([speeds, spare[:3]], axis=0), 3),
        lax.ppermute(rims, ("core", "lev"), up + down).reshape(6, 8, LANES),
    ]
    arrived = jnp.concatenate(arrived, axis=0)
    sums, energy_sums = pl.pallas_call(
        local_late_kernel,
        out_shape=(sums_shape, jax.ShapeDtypeStruct((BLOCKS, 2, 8, LANES), f32)),
        in_specs=[flag] + [VMEM] * 6,
        out_specs=(VMEM, VMEM),
        compiler_params=params,
        cost_estimate=pl.CostEstimate(flops=20_000_000, bytes_accessed=1_000_000, transcendentals=0),
        name="local_late",
    )(early, made, *operands, edges_on_cell, energy_weight)
    around = lax.all_gather(arrived, "core")
    return pl.pallas_call(
        finish_kernel,
        out_shape=(
            jax.ShapeDtypeStruct(velocity.shape, f32),
            jax.ShapeDtypeStruct(velocity.shape, f32),
            jax.ShapeDtypeStruct((velocity.shape[0], edges_on_cell.shape[1]), f32),
        ),
        in_specs=[pl.BlockSpec(memory_space=pltpu.SMEM)] + [VMEM] * 13,
        out_specs=(VMEM, VMEM, VMEM),
        scratch_shapes=[pltpu.VMEM((6, 8, LANES), f32), pltpu.VMEM((4, 8, LANES), f32)],
        compiler_params=params,
        name="finish",
    )(
        core.astype(jnp.int32).reshape(1), own, around, sums, energy_sums, edges_on_edge, weights_on_edge,
        edges_on_cell, energy_weight, cells_on_edge, inverse_distance.reshape(1, -1), vorticity,
        vertical_wind, velocity,
    )


def solution(mesh):
    fine = Mesh(mesh.devices.reshape(4, 12, 2, 8), ("x", "z", "core", "lev"))
    parts = ("x", "z", "core")
    in_specs = (
        P("lev", parts),
        P("lev", parts),
        P("lev", parts),
        P("lev", parts),
        P(None, parts),
        P(None, parts),
        P(None, parts),
        P(None, parts),
        P(None, parts),
        P(parts),
        P(parts, None),
        P(parts),
        P(parts, None),
        P(parts),
    )
    out_specs = (P("lev", parts), P("lev", parts), P("lev", parts))
    return jax.shard_map(body, mesh=fine, in_specs=in_specs, out_specs=out_specs, check_vma=False)
```
